512 devices in a mesh: gx: 64 (over z, x_lo, core), gy: 8 (over y, x_hi).
Axes of the slice: x: 4 (x_hi: 2, x_lo: 2; x = x_hi * 2 + x_lo), y: 4, z: 16, core: 2. Of those that a mesh axis runs over, the one named last changes fastest.
Arguments:
- grad_late: float32 [2, 20, 512, 1024], P(None, None, 'gx', 'gy'), may hold values from -6 to 6
- grad_early: float32 [2, 20, 512, 1024], P(None, None, 'gx', 'gy'), may hold values from -6 to 6
- accumulation: bfloat16 [4, 20, 512, 1024], P(None, None, 'gx', 'gy'), may hold values from -0.021 to 0.302, as said below
- mobility_late: bfloat16 [4, 20, 512, 1024], P(None, None, 'gx', 'gy'), may hold values from -0.25 to 1.4, as said below
- mobility_early: bfloat16 [4, 20, 512, 1024], P(None, None, 'gx', 'gy'), may hold values from -0.25 to 1.4, as said below
- trans_x: bfloat16 [20, 512, 1024], P(None, 'gx', 'gy'), may hold values from 0.0099487305 to 1
- trans_y: bfloat16 [20, 512, 1024], P(None, 'gx', 'gy'), may hold values from 0.0099487305 to 1
- trans_z: bfloat16 [20, 512, 1024], P(None, 'gx', 'gy'), may hold values from 0.0099487305 to 1
- perf_cell: int32 [64, 8, 256], P('gx', 'gy'), may hold values from 0 to 20479
- perf_well: int32 [64, 8, 256], P('gx', 'gy'), may hold values from 0 to 511
- productivity: float32 [64, 8, 256], P('gx', 'gy'), may hold values from 0.3 to 3
Outputs:
- adjoint_early: float32 [2, 20, 512, 1024], P(None, None, 'gx', 'gy')
- well_partials: float32 [4, 512], P(None, 'gx')
The draws below stay inside these ranges and needn't reach their ends.
Inputs may be any that keep to these rules, and one draw needn't show every extreme that they name: `accumulation`: off-diagonal entries c1, c2 lie within 0.021 in magnitude, diagonal entries c0, c3 from 0.05 to 0.302. `mobility_late`: off-diagonal entries b1, b2 lie within 0.25 in magnitude, diagonal entries b0, b3 from 0.6 to 1.4. `mobility_early`: off-diagonal entries b1, b2 lie within 0.25 in magnitude, diagonal entries b0, b3 from 0.6 to 1.4.
All inputs are finite; a program needn't handle non-finite values.
Results may differ from the reference program's by a relative error of at most 0.0003.
Values may be sent and summed in bfloat16 or wider, within the bound.
A program may use at most 64 MiB of HBM per device.

```python
import math
import jax
import jax.numpy as jnp
import numpy as np

NZ = 20
SWEEPS = 3
CX = 8
CY = 128
PERF_DEV = 256
NX = 512
NY = 1024
NWELLS = 512
N_GX = 64
N_GY = 8


def block_field(key, diag_low, diag_high, off_size, power):
    diag_key, off_key = jax.random.split(key)
    shape = (2, NZ, NX, NY)
    uniform_diag = jax.random.uniform(diag_key, shape, jnp.float32)
    diagonal = diag_low + (diag_high - diag_low) * uniform_diag ** power
    offdiag = jax.random.uniform(off_key, shape, jnp.float32, -off_size, off_size)
    return jnp.stack([diagonal[0], offdiag[0], offdiag[1], diagonal[1]]).astype(jnp.bfloat16)


def draw_accumulation(key, part):
    key = jax.random.fold_in(key, 11)
    return block_field(key, 0.05, 0.3, 0.02, 1.0)


def draw_mobility_late(key, part):
    key = jax.random.fold_in(key, 23)
    return block_field(key, 0.6, 1.4, 0.25, 1.0)


def draw_mobility_early(key, part):
    key = jax.random.fold_in(key, 37)
    return block_field(key, 0.6, 1.4, 0.25, 1.0)


def plant(entries, own_key, smallest, high):
    spot = [jax.random.randint(jax.random.fold_in(own_key, axis), (), 0, length) for axis, length in enumerate(entries.shape)]
    longest = entries.shape.index(max(entries.shape))
    beside = spot[:longest] + [(spot[longest] + 1) % entries.shape[longest]] + spot[longest + 1:]
    return entries.at[tuple(spot)].set(smallest).at[tuple(beside)].set(high)


def block_levels(own_key, shape, cuts, smallest, largest):
    gain = 1.0
    for position, shards_of in cuts:
        heights = jax.random.uniform(jax.random.fold_in(jax.random.fold_in(own_key, 6), position), (shards_of,), jnp.float32, smallest / len(cuts), largest / len(cuts))
        gain = gain * jnp.repeat(jnp.exp(heights), shape[position] // shards_of).reshape((-1,) + (1,) * (len(shape) - 1 - position))
    return gain


def rank_bounds(number_of, lean):
    weights = [(1 << 20) // math.isqrt(grade ** lean) + 1 for grade in range(1, number_of + 1)]
    deviation = 1 + sum(weights) // (1 << 30)
    return np.cumsum(np.array([max(1, weight // deviation) for weight in weights]))


def ranked(own_key, shape, count, skew):
    table = rank_bounds(count, skew)
    lot = jax.random.randint(jax.random.fold_in(own_key, 1), shape, 0, int(table[count - 1]))
    standing = jnp.searchsorted(jnp.asarray(table, jnp.int32), lot, side="right")
    return jax.random.permutation(jax.random.fold_in(own_key, 2), count)[standing].astype(jnp.int32)


def scatter_about(rng, extent, width, reach, cuts=(), held_as=jnp.bfloat16):
    values = width * jax.random.normal(rng, extent, jnp.float32)
    if cuts:
        values = values * block_levels(rng, extent, cuts, -0.22, 0.18)
    return jnp.clip(values, -reach, reach).astype(held_as)


def setup_inputs(seed: int = 0) -> dict:
    key_list = jax.random.split(jax.random.key(seed), 12)
    return {
        "grad_late": scatter_about(key_list[0], (2, NZ, NX, NY), 1.0, 6.0, ((2, 64), (3, 8)), jnp.float32),
        "grad_early": scatter_about(key_list[1], (2, NZ, NX, NY), 1.0, 6.0, ((2, 64), (3, 8)), jnp.float32),
        "accumulation": draw_accumulation(jax.random.fold_in(key_list[11], 71), 0),
        "mobility_late": draw_mobility_late(jax.random.fold_in(key_list[11], 71), 0),
        "mobility_early": draw_mobility_early(jax.random.fold_in(key_list[11], 71), 0),
        "trans_x": jnp.clip(jnp.exp(math.log(1.0) - 4.61031033 * jax.random.uniform(key_list[5], (NZ, NX, NY), jnp.float32) ** block_levels(key_list[5], (NZ, NX, NY), ((1, 64), (2, 8)), -0.2, 0.2)), 0.0099487305, 1.0).astype(jnp.bfloat16),
        "trans_y": jnp.clip(jnp.exp(math.log(1.0) - 4.61031033 * jax.random.uniform(key_list[6], (NZ, NX, NY), jnp.float32) ** block_levels(key_list[6], (NZ, NX, NY), ((1, 64), (2, 8)), -0.2, 0.2)), 0.0099487305, 1.0).astype(jnp.bfloat16),
        "trans_z": jnp.clip(jnp.exp(math.log(1.0) - 4.61031033 * jax.random.uniform(key_list[7], (NZ, NX, NY), jnp.float32) ** block_levels(key_list[7], (NZ, NX, NY), ((1, 64), (2, 8)), -0.2, 0.2)), 0.0099487305, 1.0).astype(jnp.bfloat16),
        "perf_cell": plant(jax.random.randint(key_list[8], (N_GX, N_GY, PERF_DEV), 0, NZ * CX * CY), jax.random.fold_in(key_list[8], 1), 0, (NZ * CX * CY) - 1).astype(jnp.int32),
        "perf_well": plant(ranked(key_list[9], (N_GX, N_GY, PERF_DEV), NWELLS, 2), jax.random.fold_in(key_list[9], 3), 0, NWELLS - 1).astype(jnp.int32),
        "productivity": jnp.clip(jnp.exp(math.log(3.0) - 2.3025851 * jax.random.uniform(key_list[10], (N_GX, N_GY, PERF_DEV), jnp.float32) ** block_levels(key_list[10], (N_GX, N_GY, PERF_DEV), ((0, 64), (1, 8)), -0.2, 0.2)), 0.3, 3.0),
    }


def transpose_apply(matrix, vector):
    return jnp.stack([matrix[0] * vector[0] + matrix[2] * vector[1], matrix[1] * vector[0] + matrix[3] * vector[1]])


def face_total(padded_x, padded_y, layer_trans):
    upper_trans = jnp.concatenate([layer_trans[1:], jnp.zeros_like(layer_trans[:1])], 0)
    return (padded_x[:, 1:-1, 1:-1] + padded_x[:, 2:, 1:-1] + padded_y[:, 1:-1, 1:-1]
            + padded_y[:, 1:-1, 2:] + layer_trans + upper_trans)


def diag_inverse(padded_x, padded_y, layer_trans, accum_full, mobility, inside):
    facesum = face_total(padded_x, padded_y, layer_trans)
    diag_block = accum_full + facesum[None] * mobility
    determinant = diag_block[0] * diag_block[3] - diag_block[1] * diag_block[2]
    determinant = jnp.where(inside > 0, determinant, jnp.float32(1.0))
    det_scale = inside / determinant
    return jnp.stack([diag_block[3] * det_scale, -diag_block[1] * det_scale,
                      -diag_block[2] * det_scale, diag_block[0] * det_scale])


def jacobi_sweep(adjoint_pad, padded_x, padded_y, layer_trans, source, mobility, inverse):
    centre = adjoint_pad[:, :, 1:-1, 1:-1]
    inflow = padded_x[None, :, 1:-1, 1:-1] * adjoint_pad[:, :, :-2, 1:-1] + padded_x[None, :, 2:, 1:-1] * adjoint_pad[:, :, 2:, 1:-1]
    inflow = inflow + padded_y[None, :, 1:-1, 1:-1] * adjoint_pad[:, :, 1:-1, :-2] + padded_y[None, :, 1:-1, 2:] * adjoint_pad[:, :, 1:-1, 2:]
    zero_layer = jnp.zeros_like(centre[:, :1])
    lower_cell = jnp.concatenate([zero_layer, centre[:, :-1]], 1)
    upper_cell = jnp.concatenate([centre[:, 1:], zero_layer], 1)
    upper_trans = jnp.concatenate([layer_trans[1:], jnp.zeros_like(layer_trans[:1])], 0)
    inflow = inflow + layer_trans[None] * lower_cell + upper_trans[None] * upper_cell
    return transpose_apply(inverse, source + transpose_apply(mobility, inflow))


def pad_lateral(array):
    widths = ((0, 0),) * (array.ndim - 2) + ((1, 1), (1, 1))
    return jnp.pad(array, widths)


def reference(grad_late, grad_early, accumulation, mobility_late, mobility_early, trans_x, trans_y, trans_z, perf_cell, perf_well, productivity):
    row_ids = jnp.arange(NX)
    col_ids = jnp.arange(NY)
    layer_ids = jnp.arange(NZ)
    masked_x = trans_x.astype(jnp.float32) * (row_ids > 0).astype(jnp.float32)[None, :, None]
    masked_y = trans_y.astype(jnp.float32) * (col_ids > 0).astype(jnp.float32)[None, None, :]
    masked_z = trans_z.astype(jnp.float32) * (layer_ids > 0).astype(jnp.float32)[:, None, None]
    padded_x = pad_lateral(masked_x)
    padded_y = pad_lateral(masked_y)
    inside = jnp.ones((NZ, NX, NY), jnp.float32)
    accum_full = accumulation.astype(jnp.float32)

    def solve(source, mobility_arg):
        mobility = mobility_arg.astype(jnp.float32)
        inverse = diag_inverse(padded_x, padded_y, masked_z, accum_full, mobility, inside)
        adjoint = transpose_apply(inverse, source)
        for sweep_index in range(SWEEPS):
            adjoint = jacobi_sweep(pad_lateral(adjoint), padded_x, padded_y, masked_z, source, mobility, inverse)
        return adjoint

    adjoint_late = solve(grad_late, mobility_late)
    adjoint_early = solve(grad_early + transpose_apply(accum_full, adjoint_late), mobility_early)
    values = jnp.concatenate([adjoint_early, adjoint_late], 0)
    values = values.reshape(4, NZ, N_GX, CX, N_GY, CY).transpose(2, 4, 0, 1, 3, 5)
    values = values.reshape(N_GX, N_GY, 4, NZ * CX * CY)
    picked = jnp.take_along_axis(values, perf_cell[:, :, None, :].astype(jnp.int32), axis=3)
    perf_terms = picked * productivity[:, :, None, :]
    perf_terms = perf_terms.transpose(0, 1, 3, 2).reshape(-1, 4)
    well_partials = jax.ops.segment_sum(perf_terms, perf_well.reshape(-1), num_segments=NWELLS).T
    return adjoint_early, well_partials
```

```python
import functools

import jax
import jax.numpy as jnp
from jax import lax
from jax.experimental import pallas as pl
from jax.experimental.pallas import tpu as pltpu
from jax.sharding import PartitionSpec as P

MESH = pl.DeviceIdType.MESH
F32 = jnp.float32
BF16 = jnp.bfloat16
SWEEPS = 3
CHUNK = 4


def lanes(shape):
    return lax.broadcasted_iota(jnp.int32, shape, len(shape) - 1)


def rows_of(shape):
    return lax.broadcasted_iota(jnp.int32, shape, len(shape) - 2)


def halves(x):
    high = x.astype(BF16)
    return high, (x - high.astype(F32)).astype(BF16)


def onehot_dot(onehot, x):
    high, low = halves(x)
    return jnp.dot(onehot, high, preferred_element_type=F32) + jnp.dot(
        onehot, low, preferred_element_type=F32
    )


def kernel(
    n_gx, n_gy, nz,
    grad_late, grad_early, accum, mob_late, mob_early, trans_x, trans_y, trans_z,
    perf_cell, perf_well, productivity,
    early_out, wells_out,
    tx, txp, ty, typ, tz, k_late, k_early, inv_early, base_late, base_early, y_a, y_b,
    sx, rx, sy, ry, h_send, h_recv,
    cell_row, col_weight, pbuf, ra, sb, rb, a_send, a_recv, b_send, b_recv,
):
    i = lax.axis_index("gx")
    j = lax.axis_index("gy")
    group = 4
    a_count = group * n_gy
    per_dev = n_gx // a_count
    planes = n_gx // group
    plane, spot = i // group, i % group
    q = spot * n_gy + j
    left_right = (
        ((i + n_gx - 1) % n_gx, j),
        ((i + 1) % n_gx, j),
        (i, (j + n_gy - 1) % n_gy),
        (i, (j + 1) % n_gy),
    )

    def a_partner(d):
        t = (q + d) % a_count
        return t, (plane * group + t // n_gy, t % n_gy)

    barrier = pltpu.get_barrier_semaphore()
    greeted = 0
    for device in left_right:
        pl.semaphore_signal(barrier, inc=1, device_id=device, device_id_type=MESH)
        greeted += 1
    for d in range(1, a_count):
        pl.semaphore_signal(barrier, inc=1, device_id=a_partner(d)[1], device_id_type=MESH)
        greeted += 1
    source_q = i // per_dev
    for p in range(planes):
        pl.semaphore_signal(
            barrier, inc=1,
            device_id=(p * group + source_q // n_gy, source_q % n_gy), device_id_type=MESH,
        )
        greeted += 1

    sub = rows_of((CHUNK, 8, 128))
    lane = lanes((CHUNK, 8, 128))
    lane1 = lanes((8, 128))
    steps = nz // CHUNK

    tz[0] = jnp.zeros((8, 128), F32)
    tz[nz] = jnp.zeros((8, 128), F32)
    first_row = jnp.where(i == 0, 0, -1)
    first_col = jnp.where(j == 0, 0, -1)

    def load_trans(s, _):
        at = pl.ds(s * CHUNK, CHUNK)
        tx[at] = jnp.where(sub == first_row, 0.0, trans_x[at].astype(F32))
        ty[at] = jnp.where(lane == first_col, 0.0, trans_y[at].astype(F32))
        return 0

    lax.fori_loop(0, steps, load_trans, 0)
    for l in range(1, nz):
        tz[l] = trans_z[l].astype(F32)

    zero = jnp.zeros((8, 128), F32)
    for buf in (y_a, y_b):
        for c in range(2):
            buf[c, 0] = zero
            buf[c, nz + 1] = zero

    cells = jnp.transpose(jnp.broadcast_to(perf_cell[0], (128, 256)))
    wells = jnp.transpose(jnp.broadcast_to(perf_well[0], (128, 256)))
    prods = jnp.transpose(jnp.broadcast_to(productivity[0], (128, 256)))
    lane_p = lanes((256, 128))
    cell_line = cells // 128
    cell_row[:, 0:128] = jnp.where(cell_line == lane_p, 1.0, 0.0).astype(BF16)
    cell_row[:, 128:256] = jnp.where(cell_line == lane_p + 128, 1.0, 0.0).astype(BF16)
    col_weight[...] = jnp.where(cells % 128 == lane_p, prods, 0.0)

    pl.semaphore_wait(barrier, greeted)

    started = []

    def exchange(r, row_first, row_last, packs):
        for c in range(2):
            for l in range(nz):
                sx[r, 0, c * nz + l] = row_first(c, l)
                sx[r, 1, c * nz + l] = row_last(c, l)
            sy[r, c] = packs(c)
        copies = []
        for k, device in enumerate(left_right):
            if k < 2:
                src, dst = sx.at[r, k], rx.at[r, 1 - k]
            else:
                src, dst = sy.at[r], ry.at[r, 3 - k]
            copy = pltpu.make_async_remote_copy(
                src_ref=src, dst_ref=dst, send_sem=h_send.at[r, k], recv_sem=h_recv.at[r, k],
                device_id=device, device_id_type=MESH,
            )
            copy.start()
            copies.append(copy)
        for copy in copies:
            copy.wait_recv()
        started.extend(copies)

    def pack(plane_of):
        out = zero
        for l in range(nz):
            rolled = pltpu.roll(plane_of(l), 1 + 2 * l, 1)
            out = jnp.where(lane1 // 2 == l, rolled, out)
        return out

    def sides(r, c):
        return jnp.where(lane1 % 2 == 0, ry[r, 0, c], ry[r, 1, c])

    def unpack(packed, s):
        return jnp.stack(
            [pltpu.roll(packed, 127 - 2 * (s * CHUNK + t), 1) for t in range(CHUNK)]
        )

    exchange(
        0,
        lambda c, l: tx[l, 0:1], lambda c, l: tx[l, 0:1],
        lambda c: pack(lambda l: ty[l]),
    )
    ty_side = sides(0, 0)

    def far_faces(s, _):
        at = pl.ds(s * CHUNK, CHUNK)
        above = rx[0, 1, at]
        txp[at] = jnp.where(sub == 7, above, pltpu.roll(tx[at], 7, 1))
        ends = unpack(ty_side, s)
        typ[at] = pltpu.roll(jnp.where(lane == 0, ends, ty[at]), 127, 2)
        return 0

    lax.fori_loop(0, steps, far_faces, 0)

    def setup(mob, k_out, inv_out, y_out, base_out, source):
        def body(s, _):
            at = pl.ds(s * CHUNK, CHUNK)
            faces = tx[at] + txp[at] + ty[at] + typ[at] + tz[at] + tz[pl.ds(s * CHUNK + 1, CHUNK)]
            b = [mob[k, at].astype(F32) for k in range(4)]
            d = [accum[k, at].astype(F32) + faces * b[k] for k in range(4)]
            scale = 1.0 / (d[0] * d[3] - d[1] * d[2])
            inv = [d[3] * scale, -d[1] * scale, -d[2] * scale, d[0] * scale]
            k_out[0, at] = inv[0] * b[0] + inv[2] * b[1]
            k_out[1, at] = inv[0] * b[2] + inv[2] * b[3]
            k_out[2, at] = inv[1] * b[0] + inv[3] * b[1]
            k_out[3, at] = inv[1] * b[2] + inv[3] * b[3]
            if inv_out is not None:
                for k in range(4):
                    inv_out[k, at] = inv[k]
            if source is not None:
                v = [source[c, at] for c in range(2)]
                at1 = pl.ds(s * CHUNK + 1, CHUNK)
                y0 = inv[0] * v[0] + inv[2] * v[1]
                y1 = inv[1] * v[0] + inv[3] * v[1]
                base_out[0, at] = y0
                base_out[1, at] = y1
                y_out[0, at1] = y0
                y_out[1, at1] = y1
            return 0

        lax.fori_loop(0, steps, body, 0)

    setup(mob_late, k_late, None, y_a, base_late, grad_late)
    setup(mob_early, k_early, inv_early, None, None, None)

    def sweep(r, y, k_mat, base, y_out, shift_out):
        exchange(
            r,
            lambda c, l: y[c, l + 1, 0:1], lambda c, l: y[c, l + 1, 7:8],
            lambda c: pack(lambda l: y[c, l + 1]),
        )
        side = [sides(r, c) for c in range(2)]

        def body(s, _):
            at = pl.ds(s * CHUNK, CHUNK)
            at1 = pl.ds(s * CHUNK + 1, CHUNK)
            at2 = pl.ds(s * CHUNK + 2, CHUNK)
            flow = []
            for c in range(2):
                mid = y[c, at1]
                below = rx[r, 0, pl.ds(c * nz + s * CHUNK, CHUNK)]
                above = rx[r, 1, pl.ds(c * nz + s * CHUNK, CHUNK)]
                ends = unpack(side[c], s)
                x_low = jnp.where(sub == 0, below, pltpu.roll(mid, 1, 1))
                x_high = jnp.where(sub == 7, above, pltpu.roll(mid, 7, 1))
                y_low = pltpu.roll(jnp.where(lane == 127, ends, mid), 1, 2)
                y_high = pltpu.roll(jnp.where(lane == 0, ends, mid), 127, 2)
                flow.append(
                    tx[at] * x_low + txp[at] * x_high + ty[at] * y_low + typ[at] * y_high
                    + tz[at] * y[c, at] + tz[at1] * y[c, at2]
                )
            for c in range(2):
                y_out[c, pl.ds(s * CHUNK + shift_out, CHUNK)] = (
                    base[c, at] + k_mat[2 * c, at] * flow[0] + k_mat[2 * c + 1, at] * flow[1]
                )
            return 0

        lax.fori_loop(0, steps, body, 0)

    sweep(1, y_a, k_late, base_late, y_b, 1)
    sweep(2, y_b, k_late, base_late, y_a, 1)
    sweep(3, y_a, k_late, base_late, y_b, 1)

    pad = jnp.zeros((256 - 8 * nz, 128), F32)

    def picked(field):
        lines = jnp.concatenate([field.reshape(8 * nz, 128), pad], 0)
        terms = onehot_dot(cell_row[...], lines) * col_weight[...]
        return jnp.sum(terms, axis=1, keepdims=True)

    own_lane = lane_p - wells % 8
    spread = jnp.zeros((256, 128), F32)
    for c in range(2):
        spread = jnp.where(own_lane == 8 * (c + 2), picked(y_b[c, pl.ds(1, nz)]), spread)

    def start_early(s, _):
        at = pl.ds(s * CHUNK, CHUNK)
        at1 = pl.ds(s * CHUNK + 1, CHUNK)
        late = [y_b[c, at1] for c in range(2)]
        a = [accum[k, at].astype(F32) for k in range(4)]
        v0 = grad_early[0, at] + a[0] * late[0] + a[2] * late[1]
        v1 = grad_early[1, at] + a[1] * late[0] + a[3] * late[1]
        y0 = inv_early[0, at] * v0 + inv_early[2, at] * v1
        y1 = inv_early[1, at] * v0 + inv_early[3, at] * v1
        base_early[0, at] = y0
        base_early[1, at] = y1
        y_a[0, at1] = y0
        y_a[1, at1] = y1
        return 0

    lax.fori_loop(0, steps, start_early, 0)
    sweep(4, y_a, k_early, base_early, y_b, 1)
    sweep(5, y_b, k_early, base_early, y_a, 1)
    sweep(6, y_a, k_early, base_early, early_out, 0)

    for c in range(2):
        spread = jnp.where(own_lane == 8 * c, picked(early_out[c]), spread)
    owner = jnp.where(
        rows_of((n_gx, 256)) == jnp.broadcast_to(perf_well[0] // 8, (n_gx, 256)), 1.0, 0.0
    ).astype(BF16)
    partial = onehot_dot(owner, spread)
    for o in range(n_gx):
        pbuf[o] = partial[o : o + 1]

    for d in range(1, a_count):
        t, device = a_partner(d)
        copy = pltpu.make_async_remote_copy(
            src_ref=pbuf.at[pl.ds(t * per_dev, per_dev)], dst_ref=ra.at[pl.ds(d * per_dev, per_dev)],
            send_sem=a_send.at[d], recv_sem=a_recv, device_id=device, device_id_type=MESH,
        )
        copy.start()
        started.append(copy)
    landed = ra.at[pl.ds(per_dev, n_gx - per_dev)]
    pltpu.make_async_copy(landed, landed, a_recv).wait()
    for r in range(per_dev):
        total = pbuf[q * per_dev + r]
        for d in range(1, a_count):
            total = total + ra[d * per_dev + r]
        sb[r] = total

    def b_copy(r, dest_j):
        dest_i = q * per_dev + r
        own = jnp.logical_and(dest_i == i, j == dest_j)
        return own, pltpu.make_async_remote_copy(
            src_ref=sb.at[r], dst_ref=rb.at[plane], send_sem=b_send.at[r * n_gy + dest_j], recv_sem=b_recv,
            device_id=(dest_i, dest_j), device_id_type=MESH,
        )

    for r in range(per_dev):
        for dest_j in range(n_gy):
            own, copy = b_copy(r, dest_j)
            pl.when(jnp.logical_not(own))(copy.start)
            pl.when(own)(pltpu.make_async_copy(sb.at[r], rb.at[plane], b_recv).start)
    pltpu.make_async_copy(rb, rb, b_recv).wait()
    total = rb[0]
    for p in range(1, planes):
        total = total + rb[p]
    total = jnp.broadcast_to(total, (8, 128))
    out = total
    for k in range(1, 4):
        out = jnp.where(rows_of((8, 128)) == k, pltpu.roll(total, 128 - 8 * k, 1), out)
    wells_out[...] = out[0:4, 0:8]

    for copy in started:
        copy.wait_send()
    for r in range(per_dev):
        for dest_j in range(n_gy):
            own, copy = b_copy(r, dest_j)
            pl.when(jnp.logical_not(own))(copy.wait_send)


def per_device(n_gx, n_gy, *args):
    nz = args[5].shape[0]
    rounds = 2 * SWEEPS + 1
    a_count = 4 * n_gy
    per_dev = n_gx // a_count
    planes = n_gx // 4
    field = pltpu.VMEM((nz, 8, 128), F32)
    field2 = pltpu.VMEM((2, nz, 8, 128), F32)
    field4 = pltpu.VMEM((4, nz, 8, 128), F32)
    padded = pltpu.VMEM((2, nz + 2, 8, 128), F32)
    dma = pltpu.SemaphoreType.DMA
    vmem = pl.BlockSpec(memory_space=pltpu.VMEM)
    return pl.pallas_call(
        functools.partial(kernel, n_gx, n_gy, nz),
        out_shape=(
            jax.ShapeDtypeStruct((2, nz, 8, 128), F32),
            jax.ShapeDtypeStruct((4, 8), F32),
        ),
        in_specs=[vmem] * 11,
        out_specs=(vmem, vmem),
        scratch_shapes=[
            field, field, field, field, pltpu.VMEM((nz + 1, 8, 128), F32),
            field4, field4, field4, field2, field2, padded, padded,
            pltpu.VMEM((rounds, 2, 2 * nz, 1, 128), F32),
            pltpu.VMEM((rounds, 2, 2 * nz, 1, 128), F32),
            pltpu.VMEM((rounds, 2, 8, 128), F32),
            pltpu.VMEM((rounds, 2, 2, 8, 128), F32),
            dma((rounds, 4)), dma((rounds, 4)),
            pltpu.VMEM((256, 256), BF16), pltpu.VMEM((256, 128), F32),
            pltpu.VMEM((n_gx, 1, 128), F32), pltpu.VMEM((n_gx, 1, 128), F32),
            pltpu.VMEM((per_dev, 1, 128), F32), pltpu.VMEM((planes, 1, 128), F32),
            dma((a_count,)), dma, dma((per_dev * n_gy,)), dma,
        ],
        compiler_params=pltpu.CompilerParams(
            collective_id=0, has_side_effects=True, vmem_limit_bytes=40 * 1024 * 1024
        ),
    )(*args)


def solution(mesh):
    n_gx, n_gy = mesh.shape["gx"], mesh.shape["gy"]
    cells = P(None, None, "gx", "gy")
    faces = P(None, "gx", "gy")
    perfs = P("gx", "gy", None)
    return jax.shard_map(
        functools.partial(per_device, n_gx, n_gy),
        mesh=mesh,
        in_specs=(cells,) * 5 + (faces,) * 3 + (perfs,) * 3,
        out_specs=(cells, P(None, "gx")),
        check_vma=False,
    )
```

```python
import functools

import jax
import jax.numpy as jnp
from jax import lax
from jax.experimental import pallas as pl
from jax.experimental.pallas import tpu as pltpu
from jax.sharding import PartitionSpec as P

MESH = pl.DeviceIdType.MESH
F32 = jnp.float32
BF16 = jnp.bfloat16
SWEEPS = 3
CHUNK = 4


def lanes(shape):
    return lax.broadcasted_iota(jnp.int32, shape, len(shape) - 1)


def rows_of(shape):
    return lax.broadcasted_iota(jnp.int32, shape, len(shape) - 2)


def halves(x):
    high = x.astype(BF16)
    return high, (x - high.astype(F32)).astype(BF16)


def onehot_dot(onehot, x):
    high, low = halves(x)
    return jnp.dot(onehot, high, preferred_element_type=F32) + jnp.dot(
        onehot, low, preferred_element_type=F32
    )


def kernel(
    n_gx, n_gy, nz,
    *refs,
):
    inputs, (early_out, wells_out) = refs[:11], refs[11:13]
    held, refs = refs[13:24], refs[24:]
    (
        in_sem,
        tx, txp, ty, typ, tz, k_late, k_early, inv_early, base_late, base_early, y_a, y_b,
        sx, rx, sy, ry, h_send, h_recv,
        cell_row, col_weight, pbuf, ra, sb, rb, a_send, a_recv, b_send, b_recv, hello,
    ) = refs
    (
        grad_late, grad_early, accum, mob_late, mob_early, trans_x, trans_y, trans_z,
        perf_cell, perf_well, productivity,
    ) = held
    i = lax.axis_index("gx")
    j = lax.axis_index("gy")
    group = 4
    a_count = group * n_gy
    per_dev = n_gx // a_count
    planes = n_gx // group
    plane, spot = i // group, i % group
    q = spot * n_gy + j
    left_right = (
        ((i + n_gx - 1) % n_gx, j),
        ((i + 1) % n_gx, j),
        (i, (j + n_gy - 1) % n_gy),
        (i, (j + 1) % n_gy),
    )

    def a_partner(d):
        t = (q + d) % a_count
        return t, (plane * group + t // n_gy, t % n_gy)

    loads = [
        pltpu.make_async_copy(inputs[k], held[k], in_sem.at[k])
        for k in (5, 6, 7, 3, 2, 0, 4, 1, 8, 9, 10)
    ]
    for load in loads:
        load.start()

    def mate(distance):
        return ((i + group * distance + n_gx) % n_gx, j)

    near = [mate(d) for d in (-3, -2, -1, 1, 2, 3)]
    far = [mate(d) for d in (-5, 5)]
    barrier = pltpu.get_barrier_semaphore()
    greeted = [*left_right[:2], *near] + [a_partner(d)[1] for d in range(1, a_count)]
    for device in greeted:
        pl.semaphore_signal(barrier, inc=1, device_id=device, device_id_type=MESH)
    for load in loads:
        load.wait()

    sub = rows_of((CHUNK, 8, 128))
    lane = lanes((CHUNK, 8, 128))
    lane1 = lanes((8, 128))
    steps = nz // CHUNK

    tz[0] = jnp.zeros((8, 128), F32)
    tz[nz] = jnp.zeros((8, 128), F32)
    first_row = jnp.where(i == 0, 0, -1)
    first_col = jnp.where(j == 0, 0, -1)

    def load_trans(s, _):
        at = pl.ds(s * CHUNK, CHUNK)
        tx[at] = jnp.where(sub == first_row, 0.0, trans_x[at].astype(F32))
        ty[at] = jnp.where(lane == first_col, 0.0, trans_y[at].astype(F32))
        return 0

    lax.fori_loop(0, steps, load_trans, 0)
    for l in range(1, nz):
        tz[l] = trans_z[l].astype(F32)

    zero = jnp.zeros((8, 128), F32)
    for buf in (y_a, y_b):
        for c in range(2):
            buf[c, 0] = zero
            buf[c, nz + 1] = zero

    cells = jnp.transpose(jnp.broadcast_to(perf_cell[0], (128, 256)))
    wells = jnp.transpose(jnp.broadcast_to(perf_well[0], (128, 256)))
    prods = jnp.transpose(jnp.broadcast_to(productivity[0], (128, 256)))
    lane_p = lanes((256, 128))
    cell_line = cells // 128
    cell_row[:, 0:128] = jnp.where(cell_line == lane_p, 1.0, 0.0).astype(BF16)
    cell_row[:, 128:256] = jnp.where(cell_line == lane_p + 128, 1.0, 0.0).astype(BF16)
    col_weight[...] = jnp.where(cells % 128 == lane_p, prods, 0.0)

    pl.semaphore_wait(barrier, len(greeted))
    for device in near:
        pl.semaphore_signal(hello.at[0], inc=1, device_id=device, device_id_type=MESH)

    started = []

    def exchange(r, row_first, row_last, packs):
        for c in range(2):
            for l in range(nz):
                sx[r, 0, c * nz + l] = row_first(c, l)
                sx[r, 1, c * nz + l] = row_last(c, l)
            sy[r, c] = packs(c)
        copies = []
        for k, device in enumerate(left_right):
            if k < 2:
                src, dst = sx.at[r, k], rx.at[r, 1 - k]
            else:
                src, dst = sy.at[r], ry.at[r, 3 - k]
            copy = pltpu.make_async_remote_copy(
                src_ref=src, dst_ref=dst, send_sem=h_send.at[r, k], recv_sem=h_recv.at[r, k],
                device_id=device, device_id_type=MESH,
            )
            copy.start()
            copies.append(copy)
        for copy in copies:
            copy.wait_recv()
        started.extend(copies)

    def pack(plane_of):
        out = zero
        for l in range(nz):
            rolled = pltpu.roll(plane_of(l), 1 + 2 * l, 1)
            out = jnp.where(lane1 // 2 == l, rolled, out)
        return out

    def sides(r, c):
        return jnp.where(lane1 % 2 == 0, ry[r, 0, c], ry[r, 1, c])

    def unpack(packed, s):
        return jnp.stack(
            [pltpu.roll(packed, 127 - 2 * (s * CHUNK + t), 1) for t in range(CHUNK)]
        )

    exchange(
        0,
        lambda c, l: tx[l, 0:1], lambda c, l: tx[l, 0:1],
        lambda c: pack(lambda l: ty[l]),
    )
    ty_side = sides(0, 0)

    def far_faces(s, _):
        at = pl.ds(s * CHUNK, CHUNK)
        above = rx[0, 1, at]
        txp[at] = jnp.where(sub == 7, above, pltpu.roll(tx[at], 7, 1))
        ends = unpack(ty_side, s)
        typ[at] = pltpu.roll(jnp.where(lane == 0, ends, ty[at]), 127, 2)
        return 0

    lax.fori_loop(0, steps, far_faces, 0)

    def setup(mob, k_out, inv_out, y_out, base_out, source):
        def body(s, _):
            at = pl.ds(s * CHUNK, CHUNK)
            faces = tx[at] + txp[at] + ty[at] + typ[at] + tz[at] + tz[pl.ds(s * CHUNK + 1, CHUNK)]
            b = [mob[k, at].astype(F32) for k in range(4)]
            d = [accum[k, at].astype(F32) + faces * b[k] for k in range(4)]
            scale = 1.0 / (d[0] * d[3] - d[1] * d[2])
            inv = [d[3] * scale, -d[1] * scale, -d[2] * scale, d[0] * scale]
            k_out[0, at] = inv[0] * b[0] + inv[2] * b[1]
            k_out[1, at] = inv[0] * b[2] + inv[2] * b[3]
            k_out[2, at] = inv[1] * b[0] + inv[3] * b[1]
            k_out[3, at] = inv[1] * b[2] + inv[3] * b[3]
            if inv_out is not None:
                for k in range(4):
                    inv_out[k, at] = inv[k]
            if source is not None:
                v = [source[c, at] for c in range(2)]
                at1 = pl.ds(s * CHUNK + 1, CHUNK)
                y0 = inv[0] * v[0] + inv[2] * v[1]
                y1 = inv[1] * v[0] + inv[3] * v[1]
                base_out[0, at] = y0
                base_out[1, at] = y1
                y_out[0, at1] = y0
                y_out[1, at1] = y1
            return 0

        lax.fori_loop(0, steps, body, 0)

    setup(mob_late, k_late, None, y_a, base_late, grad_late)
    setup(mob_early, k_early, inv_early, None, None, None)

    def sweep(r, y, k_mat, base, y_out, shift_out):
        exchange(
            r,
            lambda c, l: y[c, l + 1, 0:1], lambda c, l: y[c, l + 1, 7:8],
            lambda c: pack(lambda l: y[c, l + 1]),
        )
        side = [sides(r, c) for c in range(2)]

        def body(s, _):
            at = pl.ds(s * CHUNK, CHUNK)
            at1 = pl.ds(s * CHUNK + 1, CHUNK)
            at2 = pl.ds(s * CHUNK + 2, CHUNK)
            flow = []
            for c in range(2):
                mid = y[c, at1]
                below = rx[r, 0, pl.ds(c * nz + s * CHUNK, CHUNK)]
                above = rx[r, 1, pl.ds(c * nz + s * CHUNK, CHUNK)]
                ends = unpack(side[c], s)
                x_low = jnp.where(sub == 0, below, pltpu.roll(mid, 1, 1))
                x_high = jnp.where(sub == 7, above, pltpu.roll(mid, 7, 1))
                y_low = pltpu.roll(jnp.where(lane == 127, ends, mid), 1, 2)
                y_high = pltpu.roll(jnp.where(lane == 0, ends, mid), 127, 2)
                flow.append(
                    tx[at] * x_low + txp[at] * x_high + ty[at] * y_low + typ[at] * y_high
                    + tz[at] * y[c, at] + tz[at1] * y[c, at2]
                )
            for c in range(2):
                y_out[c, pl.ds(s * CHUNK + shift_out, CHUNK)] = (
                    base[c, at] + k_mat[2 * c, at] * flow[0] + k_mat[2 * c + 1, at] * flow[1]
                )
            return 0

        lax.fori_loop(0, steps, body, 0)

    pl.semaphore_wait(hello.at[0], len(near))
    for device in far:
        pl.semaphore_signal(hello.at[1], inc=1, device_id=device, device_id_type=MESH)
    sweep(1, y_a, k_late, base_late, y_b, 1)
    sweep(2, y_b, k_late, base_late, y_a, 1)
    sweep(3, y_a, k_late, base_late, y_b, 1)

    pad = jnp.zeros((256 - 8 * nz, 128), F32)

    def picked(field):
        lines = jnp.concatenate([field.reshape(8 * nz, 128), pad], 0)
        terms = onehot_dot(cell_row[...], lines) * col_weight[...]
        return jnp.sum(terms, axis=1, keepdims=True)

    own_lane = lane_p - wells % 8
    spread = jnp.zeros((256, 128), F32)
    for c in range(2):
        spread = jnp.where(own_lane == 8 * (c + 2), picked(y_b[c, pl.ds(1, nz)]), spread)

    def start_early(s, _):
        at = pl.ds(s * CHUNK, CHUNK)
        at1 = pl.ds(s * CHUNK + 1, CHUNK)
        late = [y_b[c, at1] for c in range(2)]
        a = [accum[k, at].astype(F32) for k in range(4)]
        v0 = grad_early[0, at] + a[0] * late[0] + a[2] * late[1]
        v1 = grad_early[1, at] + a[1] * late[0] + a[3] * late[1]
        y0 = inv_early[0, at] * v0 + inv_early[2, at] * v1
        y1 = inv_early[1, at] * v0 + inv_early[3, at] * v1
        base_early[0, at] = y0
        base_early[1, at] = y1
        y_a[0, at1] = y0
        y_a[1, at1] = y1
        return 0

    lax.fori_loop(0, steps, start_early, 0)
    sweep(4, y_a, k_early, base_early, y_b, 1)
    sweep(5, y_b, k_early, base_early, y_a, 1)
    sweep(6, y_a, k_early, base_early, early_out, 0)

    for c in range(2):
        spread = jnp.where(own_lane == 8 * c, picked(early_out[c]), spread)
    owner = jnp.where(
        rows_of((n_gx, 256)) == jnp.broadcast_to(perf_well[0] // 8, (n_gx, 256)), 1.0, 0.0
    ).astype(BF16)
    partial = onehot_dot(owner, spread)
    for o in range(n_gx):
        pbuf[o] = partial[o : o + 1]

    for d in range(1, a_count):
        t, device = a_partner(d)
        copy = pltpu.make_async_remote_copy(
            src_ref=pbuf.at[pl.ds(t * per_dev, per_dev)], dst_ref=ra.at[pl.ds(d * per_dev, per_dev)],
            send_sem=a_send.at[d], recv_sem=a_recv, device_id=device, device_id_type=MESH,
        )
        copy.start()
        started.append(copy)
    landed = ra.at[pl.ds(per_dev, n_gx - per_dev)]
    pltpu.make_async_copy(landed, landed, a_recv).wait()
    for r in range(per_dev):
        total = pbuf[q * per_dev + r]
        for d in range(1, a_count):
            total = total + ra[d * per_dev + r]
        sb[r] = total

    pl.semaphore_wait(hello.at[1], len(far))
    def b_copy(r, dest_j):
        dest_i = q * per_dev + r
        own = jnp.logical_and(dest_i == i, j == dest_j)
        return own, pltpu.make_async_remote_copy(
            src_ref=sb.at[r], dst_ref=rb.at[plane], send_sem=b_send.at[r * n_gy + dest_j], recv_sem=b_recv,
            device_id=(dest_i, dest_j), device_id_type=MESH,
        )

    for r in range(per_dev):
        for dest_j in range(n_gy):
            own, copy = b_copy(r, dest_j)
            pl.when(jnp.logical_not(own))(copy.start)
            pl.when(own)(pltpu.make_async_copy(sb.at[r], rb.at[plane], b_recv).start)
    pltpu.make_async_copy(rb, rb, b_recv).wait()
    total = rb[0]
    for p in range(1, planes):
        total = total + rb[p]
    total = jnp.broadcast_to(total, (8, 128))
    out = total
    for k in range(1, 4):
        out = jnp.where(rows_of((8, 128)) == k, pltpu.roll(total, 128 - 8 * k, 1), out)
    wells_out[...] = out[0:4, 0:8]

    for copy in started:
        copy.wait_send()
    for r in range(per_dev):
        for dest_j in range(n_gy):
            own, copy = b_copy(r, dest_j)
            pl.when(jnp.logical_not(own))(copy.wait_send)


def per_device(n_gx, n_gy, *args):
    nz = args[5].shape[0]
    rounds = 2 * SWEEPS + 1
    a_count = 4 * n_gy
    per_dev = n_gx // a_count
    planes = n_gx // 4
    field = pltpu.VMEM((nz, 8, 128), F32)
    field2 = pltpu.VMEM((2, nz, 8, 128), F32)
    field4 = pltpu.VMEM((4, nz, 8, 128), F32)
    padded = pltpu.VMEM((2, nz + 2, 8, 128), F32)
    dma = pltpu.SemaphoreType.DMA
    vmem = pl.BlockSpec(memory_space=pltpu.VMEM)
    return pl.pallas_call(
        functools.partial(kernel, n_gx, n_gy, nz),
        out_shape=(
            jax.ShapeDtypeStruct((2, nz, 8, 128), F32),
            jax.ShapeDtypeStruct((4, 8), F32),
        ),
        in_specs=[pl.BlockSpec(memory_space=pltpu.HBM)] * 11,
        out_specs=(vmem, vmem),
        scratch_shapes=[pltpu.VMEM(a.shape, a.dtype) for a in args] + [
            dma((11,)),
            field, field, field, field, pltpu.VMEM((nz + 1, 8, 128), F32),
            field4, field4, field4, field2, field2, padded, padded,
            pltpu.VMEM((rounds, 2, 2 * nz, 1, 128), F32),
            pltpu.VMEM((rounds, 2, 2 * nz, 1, 128), F32),
            pltpu.VMEM((rounds, 2, 8, 128), F32),
            pltpu.VMEM((rounds, 2, 2, 8, 128), F32),
            dma((rounds, 4)), dma((rounds, 4)),
            pltpu.VMEM((256, 256), BF16), pltpu.VMEM((256, 128), F32),
            pltpu.VMEM((n_gx, 1, 128), F32), pltpu.VMEM((n_gx, 1, 128), F32),
            pltpu.VMEM((per_dev, 1, 128), F32), pltpu.VMEM((planes, 1, 128), F32),
            dma((a_count,)), dma, dma((per_dev * n_gy,)), dma,
            pltpu.SemaphoreType.REGULAR((2,)),
        ],
        compiler_params=pltpu.CompilerParams(
            collective_id=0, has_side_effects=True, vmem_limit_bytes=60 * 1024 * 1024
        ),
    )(*args)


def solution(mesh):
    n_gx, n_gy = mesh.shape["gx"], mesh.shape["gy"]
    cells = P(None, None, "gx", "gy")
    faces = P(None, "gx", "gy")
    perfs = P("gx", "gy", None)
    return jax.shard_map(
        functools.partial(per_device, n_gx, n_gy),
        mesh=mesh,
        in_specs=(cells,) * 5 + (faces,) * 3 + (perfs,) * 3,
        out_specs=(cells, P(None, "gx")),
        check_vma=False,
    )
```

```python
import functools

import jax
import jax.numpy as jnp
from jax import lax
from jax.experimental import pallas as pl
from jax.experimental.pallas import tpu as pltpu
from jax.sharding import PartitionSpec as P

MESH = pl.DeviceIdType.MESH
F32 = jnp.float32
BF16 = jnp.bfloat16
PACK = 4
CHUNK = 2
WIDE = 6


def iota(shape, dim):
    return lax.broadcasted_iota(jnp.int32, shape, dim)


def onehot_dot(onehot, x):
    high = x.astype(BF16)
    low = (x - high.astype(F32)).astype(BF16)
    return jnp.dot(onehot, high, preferred_element_type=F32) + jnp.dot(
        onehot, low, preferred_element_type=F32
    )


def sub_of(x):
    return iota(x.shape, x.ndim - 2)


def row_shift(a, b, amount):
    ra, rb = pltpu.roll(a, amount, a.ndim - 2), pltpu.roll(b, amount, b.ndim - 2)
    edge = sub_of(a) == (0 if amount == 1 else 7)
    return jnp.where(edge, rb, ra), jnp.where(edge, ra, rb)


def pack_rows(x):
    x = x.reshape(x.shape[0] // 2, 2, 8, 128)
    even, odd = x[:, 0], pltpu.roll(x[:, 1], 4, 1)
    first = sub_of(even) < 4
    return jnp.where(first, odd, even), jnp.where(first, even, odd)


def unpack_rows(low, high):
    first = sub_of(low) < 4
    even = jnp.where(first, high, low)
    odd = pltpu.roll(jnp.where(first, low, high), 4, 1)
    return jnp.stack([even, odd], 1).reshape(2 * low.shape[0], 8, 128)


def block_system(accum, mob, faces, live=None):
    d = [accum[k] + faces * mob[k] for k in range(4)]
    det = d[0] * d[3] - d[1] * d[2]
    if live is not None:
        det = jnp.where(live, det, 1.0)
    scale = 1.0 / det
    inv = [d[3] * scale, -d[1] * scale, -d[2] * scale, d[0] * scale]
    b = mob
    mat = [
        inv[0] * b[0] + inv[2] * b[1],
        inv[0] * b[2] + inv[2] * b[3],
        inv[1] * b[0] + inv[3] * b[1],
        inv[1] * b[2] + inv[3] * b[3],
    ]
    return inv, mat


def transpose_apply(m, v):
    return [m[0] * v[0] + m[2] * v[1], m[1] * v[0] + m[3] * v[1]]


def kernel(n_gx, n_gy, nz, *refs):
    inputs, (early_out, wells_out), held = refs[:11], refs[11:13], refs[13:24]
    (
        in_sem, tx, txp, ty, typ, tz, k_late, k_early, inv_early, base_late, base_early, y_a, y_b,
        rim_faces, rim_k_late, rim_k_early, rim_late, rim_early, rim_a, rim_b,
        xs_bf, xs_f, xs_me, xs_e, xr_bf, xr_f, xr_me, xr_e, x_send, x_recv,
        ys_bf, ys_f, ys_me, ys_e, yr_bf, yr_f, yr_me, yr_e, y_send, y_recv,
        cell_row, col_weight, pbuf, ra, sb, rb, a_send, a_recv, b_send, b_recv, hello,
    ) = refs[24:]
    (
        grad_late, grad_early, accum, mob_late, mob_early, trans_x, trans_y, trans_z,
        perf_cell, perf_well, productivity,
    ) = held
    i = lax.axis_index("gx")
    j = lax.axis_index("gy")
    group = 4
    a_count = group * n_gy
    per_dev = n_gx // a_count
    planes = n_gx // group
    plane, spot = i // group, i % group
    q = spot * n_gy + j
    lower, upper = (i + n_gx - 1) % n_gx, (i + 1) % n_gx
    left, right = (j + n_gy - 1) % n_gy, (j + 1) % n_gy
    row_peers = ((upper, j), (lower, j))
    col_peers = ((i, right), (i, left), (lower, right), (lower, left), (upper, right), (upper, left))

    def a_partner(d):
        t = (q + d) % a_count
        return t, (plane * group + t // n_gy, t % n_gy)

    loads = [
        pltpu.make_async_copy(inputs[k], held[k], in_sem.at[k])
        for k in (5, 6, 7, 3, 2, 0, 4, 1, 8, 9, 10)
    ]
    for load in loads:
        load.start()

    def mate(distance):
        return ((i + group * distance + n_gx) % n_gx, j)

    near = [mate(d) for d in (-3, -2, -1, 1, 2, 3)]
    far = [mate(d) for d in (-5, 5)]
    barrier = pltpu.get_barrier_semaphore()
    greeted = [*row_peers, *col_peers, *near] + [a_partner(d)[1] for d in range(1, a_count)]
    for device in greeted:
        pl.semaphore_signal(barrier, inc=1, device_id=device, device_id_type=MESH)
    for load in loads:
        load.wait()

    zero = jnp.zeros((8, 128), F32)
    lane1 = iota((8, 128), 1)
    sub1 = iota((8, 128), 0)
    layer_of = lane1 // WIDE
    col_of = lane1 % WIDE
    live = lane1 < WIDE * nz
    packs = nz // PACK
    steps = nz // CHUNK
    first_row = jnp.where(i == 0, 0, -1)
    first_col = jnp.where(j == 0, 0, -1)

    def pack_cols(old, x, layer, extra=3):
        return jnp.where(layer_of == layer, pltpu.roll(x, extra + WIDE * layer, 1), old)

    def put_rows(x, s, send, k):
        last, first = pack_rows(x)
        if send.dtype == BF16:
            send[0, k, s] = last.reshape(4 * PACK, 128).astype(BF16)
            send[1, k, s] = first.reshape(4 * PACK, 128).astype(BF16)
        else:
            send[0, k, pl.ds(2 * s, 2)] = last
            send[1, k, pl.ds(2 * s, 2)] = first

    def first_out(s, cols):
        at = pl.ds(s * PACK, PACK)
        row, col = iota((PACK, 8, 128), 1), iota((PACK, 8, 128), 2)
        fx = jnp.where(row == first_row, 0.0, trans_x[at].astype(F32))
        fy = jnp.where(col == first_col, 0.0, trans_y[at].astype(F32))
        fz = jnp.where(iota((PACK, 8, 128), 0) + s * PACK == 0, 0.0, trans_z[at].astype(F32))
        tx[0, at] = fx
        ty[0, at] = fy
        tz[0, at] = fz
        fields = [mob_late[k, at].astype(F32) for k in range(4)]
        fields += [accum[k, at].astype(F32) for k in range(4)] + [fx, fy, fz]
        for k, x in enumerate(fields):
            put_rows(x, s, xs_bf, k)
        grads = [grad_late[c, at] for c in range(2)]
        for k, x in enumerate(grads):
            put_rows(x, s, xs_f, k)
        early = [mob_early[k, at].astype(F32) for k in range(4)]
        for k, x in enumerate(early):
            put_rows(x, s, xs_me, k)
        cols = list(cols)
        for t in range(PACK):
            layer = s * PACK + t
            for k, x in enumerate(fields + [fy] + grads + early):
                cols[k] = pack_cols(cols[k], x[t], layer, 2 if k == 11 else 3)
        return tuple(cols)

    cols = lax.fori_loop(0, packs, first_out, (zero,) * 18)
    for k in range(6):
        ys_bf[k] = jnp.concatenate([cols[2 * k], cols[2 * k + 1]], 0).astype(BF16)
    for k in range(2):
        ys_f[k] = cols[12 + k]
        ys_me[k] = jnp.concatenate([cols[14 + 2 * k], cols[15 + 2 * k]], 0).astype(BF16)

    pl.semaphore_wait(barrier, len(greeted))

    started = []

    def send(kind, x_src, x_dst, y_src, y_dst):
        copies = []
        for k, device in enumerate(row_peers):
            copies.append(pltpu.make_async_remote_copy(
                src_ref=x_src.at[k], dst_ref=x_dst.at[k], send_sem=x_send.at[kind, k],
                recv_sem=x_recv.at[kind, k], device_id=device, device_id_type=MESH,
            ))
        for k, device in enumerate(col_peers):
            copies.append(pltpu.make_async_remote_copy(
                src_ref=y_src, dst_ref=y_dst.at[k], send_sem=y_send.at[kind, k],
                recv_sem=y_recv.at[kind, k], device_id=device, device_id_type=MESH,
            ))
        for copy in copies:
            copy.start()
        started.extend(copies)
        return copies

    def arrived(copies):
        for copy in copies:
            copy.wait_recv()

    sent_bf = send(0, xs_bf, xr_bf, ys_bf, yr_bf)
    sent_f = send(1, xs_f, xr_f, ys_f, yr_f)
    sent_me = send(2, xs_me, xr_me, ys_me, yr_me)

    for device in near:
        pl.semaphore_signal(hello.at[0], inc=1, device_id=device, device_id_type=MESH)

    cells = jnp.transpose(jnp.broadcast_to(perf_cell[0], (128, 256)))
    wells = jnp.transpose(jnp.broadcast_to(perf_well[0], (128, 256)))
    prods = jnp.transpose(jnp.broadcast_to(productivity[0], (128, 256)))
    lane_p = iota((256, 128), 1)
    cell_line = cells // 128
    cell_row[:, 0:128] = jnp.where(cell_line == lane_p, 1.0, 0.0).astype(BF16)
    cell_row[:, 128:256] = jnp.where(cell_line == lane_p + 128, 1.0, 0.0).astype(BF16)
    col_weight[...] = jnp.where(cells % 128 == lane_p, prods, 0.0)
    for block in range(2):
        tz[block, nz] = zero
        for buf in (y_a, y_b):
            for c in range(2):
                buf[block, c, 0] = zero
                buf[block, c, nz + 1] = zero

    def get_rows(recv, k, s):
        if recv.dtype == BF16:
            low, high = (recv[d, k, s].astype(F32).reshape(2, 8, 128) for d in range(2))
        else:
            low, high = (recv[d, k, pl.ds(2 * s, 2)] for d in range(2))
        return unpack_rows(low, high)

    def rim(recv, k):
        if recv.dtype == BF16:
            part = [recv[d, k // 2, 0:16].astype(F32)[8 * (k % 2) : 8 * (k % 2) + 8] for d in range(6)]
        else:
            part = [recv[d, k] for d in range(6)]
        beside, up, down = (jnp.where(col_of < 3, part[d], part[d + 1]) for d in (0, 2, 4))
        return beside, jnp.where(sub1 < 4, up, down)

    arrived(sent_bf)

    def rim_trans(s, old):
        at = pl.ds(s * PACK, PACK)
        tx[1, at] = get_rows(xr_bf, 8, s)
        fy = get_rows(xr_bf, 9, s)
        ty[1, at] = fy
        tz[1, at] = get_rows(xr_bf, 10, s)
        for t in range(PACK):
            old = pack_cols(old, fy[t], s * PACK + t)
        return old

    ty_cols = (cols[9], lax.fori_loop(0, packs, rim_trans, zero))
    rim_tx, rim_ty, rim_tz, rim_typ = (rim(yr_bf, k) for k in (8, 9, 10, 11))
    rim_txp = row_shift(*rim_tx, 7)
    rim_all = []
    for block in range(2):
        at_edge = pltpu.roll(ty_cols[block], 127, 1)
        faces = [
            rim_tx[block], rim_txp[block], rim_ty[block],
            jnp.where(col_of == 2, at_edge, rim_typ[block]),
            rim_tz[block], pltpu.roll(rim_tz[block], 128 - WIDE, 1),
        ]
        for k in range(6):
            rim_faces[k, block] = faces[k]
        rim_all.append(faces[0] + faces[1] + faces[2] + faces[3] + faces[4] + faces[5])

    def ends(packed, s):
        return jnp.stack([pltpu.roll(packed, 125 - WIDE * (s * CHUNK + t), 1) for t in range(CHUNK)])

    def faces_late(s, cols):
        cols = [list(c) for c in cols]
        at4 = pl.ds(s * PACK, PACK)
        rim_mob = [get_rows(xr_bf, k, s) for k in range(4)]
        rim_acc = [get_rows(xr_bf, 4 + k, s) for k in range(4)]
        rim_grad = [get_rows(xr_f, c, s) for c in range(2)]
        for h in range(PACK // CHUNK):
            part = slice(h * CHUNK, (h + 1) * CHUNK)
            step = s * (PACK // CHUNK) + h
            at = pl.ds(step * CHUNK, CHUNK)
            after = pl.ds(step * CHUNK + 1, CHUNK)
            lane = iota((CHUNK, 8, 128), 2)
            far_x = row_shift(tx[0, at], tx[1, at], 7)
            for block in range(2):
                fy = ty[block, at]
                far_y = pltpu.roll(jnp.where(lane == 0, ends(rim_ty[block], step), fy), 127, 2)
                txp[block, at] = far_x[block]
                typ[block, at] = far_y
                faces = tx[block, at] + far_x[block] + fy + far_y + tz[block, at] + tz[block, after]
                if block == 0:
                    mob = [mob_late[k, at].astype(F32) for k in range(4)]
                    acc = [accum[k, at].astype(F32) for k in range(4)]
                    grad = [grad_late[c, at] for c in range(2)]
                else:
                    mob, acc, grad = ([x[part] for x in f] for f in (rim_mob, rim_acc, rim_grad))
                inv, mat = block_system(acc, mob, faces)
                for k in range(4):
                    k_late[block, k, at] = mat[k]
                first = transpose_apply(inv, grad)
                for c in range(2):
                    base_late[block, c, at] = first[c]
                    y_a[block, c, after] = first[c]
                    for t in range(CHUNK):
                        cols[block][c] = pack_cols(cols[block][c], first[c][t], step * CHUNK + t)
                if block == 0:
                    mob = [mob_early[k, at].astype(F32) for k in range(4)]
                    inv, mat = block_system(acc, mob, faces)
                    for k in range(4):
                        k_early[0, k, at] = mat[k]
                        inv_early[k, at] = inv[k]
        return tuple(tuple(c) for c in cols)

    arrived(sent_f)
    cols_none = ((zero, zero), (zero, zero))
    late_cols = lax.fori_loop(0, packs, faces_late, cols_none)
    rim_acc_y = [rim(yr_bf, 4 + k) for k in range(4)]
    rim_mob_y = [rim(yr_bf, k) for k in range(4)]
    rim_grad_y = [rim(yr_f, c) for c in range(2)]
    for block in range(2):
        inv, mat = block_system(
            [x[block] for x in rim_acc_y], [x[block] for x in rim_mob_y], rim_all[block], live
        )
        first = transpose_apply(inv, [x[block] for x in rim_grad_y])
        for k in range(4):
            rim_k_late[block, k] = mat[k]
        for c in range(2):
            rim_late[block, c] = first[c]
            rim_a[block, c] = first[c]

    def sweep(cols, y, rim_y, mats, base, rim_mats, rim_base, y_out, rim_out, last=False):
        old = [[rim_y[block, c] for c in range(2)] for block in range(2)]
        blocks = (0,) if last else (0, 1)

        def body(s, packed):
            packed = [list(p) for p in packed]
            at = pl.ds(s * CHUNK, CHUNK)
            at1 = pl.ds(s * CHUNK + 1, CHUNK)
            at2 = pl.ds(s * CHUNK + 2, CHUNK)
            lane = iota((CHUNK, 8, 128), 2)
            flow = [[], []]
            for c in range(2):
                mid = [y[block, c, at1] for block in range(2)]
                below = row_shift(*mid, 1)
                above = row_shift(*mid, 7)
                for block in blocks:
                    side = ends(old[block][c], s)
                    y_low = pltpu.roll(jnp.where(lane == 127, side, mid[block]), 1, 2)
                    y_high = pltpu.roll(jnp.where(lane == 0, side, mid[block]), 127, 2)
                    flow[block].append(
                        tx[block, at] * below[block] + txp[block, at] * above[block]
                        + ty[block, at] * y_low + typ[block, at] * y_high
                        + tz[block, at] * y[block, c, at] + tz[block, at1] * y[block, c, at2]
                    )
            for block in blocks:
                for c in range(2):
                    new = (
                        base[block, c, at] + mats[block, 2 * c, at] * flow[block][0]
                        + mats[block, 2 * c + 1, at] * flow[block][1]
                    )
                    if last:
                        y_out(c, s, new)
                    else:
                        y_out[block, c, at1] = new
                        for t in range(CHUNK):
                            packed[block][c] = pack_cols(packed[block][c], new[t], s * CHUNK + t)
            return tuple(tuple(p) for p in packed)

        packed = lax.fori_loop(0, steps, body, cols_none)
        if last:
            return None
        flow = [[], []]
        for c in range(2):
            below = row_shift(old[0][c], old[1][c], 1)
            above = row_shift(old[0][c], old[1][c], 7)
            for block in range(2):
                mid, own = old[block][c], cols[block][c]
                f = [rim_faces[k, block] for k in range(6)]
                flow[block].append(
                    f[0] * below[block] + f[1] * above[block]
                    + f[2] * pltpu.roll(jnp.where(col_of == 2, own, mid), 1, 1)
                    + f[3] * pltpu.roll(jnp.where(col_of == 3, own, mid), 127, 1)
                    + f[4] * pltpu.roll(mid, WIDE, 1) + f[5] * pltpu.roll(mid, 128 - WIDE, 1)
                )
        for block in range(2):
            for c in range(2):
                rim_out[block, c] = (
                    rim_base[block, c] + rim_mats[block, 2 * c] * flow[block][0]
                    + rim_mats[block, 2 * c + 1] * flow[block][1]
                )
        return packed

    late_args = (k_late, base_late, rim_k_late, rim_late)
    late_cols = sweep(late_cols, y_a, rim_a, *late_args, y_b, rim_b)
    late_cols = sweep(late_cols, y_b, rim_b, *late_args, y_a, rim_a)

    def keep_late(c, s, new):
        y_b[0, c, pl.ds(s * CHUNK + 1, CHUNK)] = new

    sweep(late_cols, y_a, rim_a, *late_args, keep_late, None, last=True)

    def start_early(s, cols):
        cols = list(cols)
        at = pl.ds(s * PACK, PACK)
        at1 = pl.ds(s * PACK + 1, PACK)
        late = [y_b[0, c, at1] for c in range(2)]
        more = transpose_apply([accum[k, at].astype(F32) for k in range(4)], late)
        source = [grad_early[c, at] + more[c] for c in range(2)]
        first = transpose_apply([inv_early[k, at] for k in range(4)], source)
        for c in range(2):
            base_early[0, c, at] = first[c]
            y_a[0, c, at1] = first[c]
            put_rows(first[c], s, xs_e, c)
            for t in range(PACK):
                cols[c] = pack_cols(cols[c], first[c][t], s * PACK + t)
        return tuple(cols)

    own_cols = lax.fori_loop(0, packs, start_early, (zero, zero))
    for c in range(2):
        ys_e[c] = own_cols[c]
    sent_e = send(3, xs_e, xr_e, ys_e, yr_e)

    pl.semaphore_wait(hello.at[0], len(near))
    for device in far:
        pl.semaphore_signal(hello.at[1], inc=1, device_id=device, device_id_type=MESH)
    arrived(sent_me)

    def rim_early_mats(s, _):
        rim_mob = [get_rows(xr_me, k, s) for k in range(4)]
        rim_acc = [get_rows(xr_bf, 4 + k, s) for k in range(4)]
        at = pl.ds(s * PACK, PACK)
        after = pl.ds(s * PACK + 1, PACK)
        faces = tx[1, at] + txp[1, at] + ty[1, at] + typ[1, at] + tz[1, at] + tz[1, after]
        _, mat = block_system(rim_acc, rim_mob, faces)
        for k in range(4):
            k_early[1, k, at] = mat[k]
        return 0

    lax.fori_loop(0, packs, rim_early_mats, 0)
    rim_mob_y = [rim(yr_me, k) for k in range(4)]
    for block in range(2):
        _, mat = block_system(
            [x[block] for x in rim_acc_y], [x[block] for x in rim_mob_y], rim_all[block], live
        )
        for k in range(4):
            rim_k_early[block, k] = mat[k]

    pad = jnp.zeros((256 - 8 * nz, 128), F32)

    def picked(field):
        lines = jnp.concatenate([field.reshape(8 * nz, 128), pad], 0)
        terms = onehot_dot(cell_row[...], lines) * col_weight[...]
        return jnp.sum(terms, axis=1, keepdims=True)

    own_lane = lane_p - wells % 8
    spread = jnp.zeros((256, 128), F32)
    for c in range(2):
        spread = jnp.where(own_lane == 8 * (c + 2), picked(y_b[0, c, pl.ds(1, nz)]), spread)
    owner = jnp.where(
        iota((n_gx, 256), 0) == jnp.broadcast_to(perf_well[0] // 8, (n_gx, 256)), 1.0, 0.0
    ).astype(BF16)

    arrived(sent_e)

    def rim_start(s, cols):
        cols = list(cols)
        at = pl.ds(s * PACK, PACK)
        at1 = pl.ds(s * PACK + 1, PACK)
        for c in range(2):
            first = get_rows(xr_e, c, s)
            base_early[1, c, at] = first
            y_a[1, c, at1] = first
            for t in range(PACK):
                cols[c] = pack_cols(cols[c], first[t], s * PACK + t)
        return tuple(cols)

    early_cols = (own_cols, lax.fori_loop(0, packs, rim_start, (zero, zero)))
    for c in range(2):
        pair = rim(yr_e, c)
        for block in range(2):
            rim_early[block, c] = pair[block]
            rim_a[block, c] = pair[block]

    early_args = (k_early, base_early, rim_k_early, rim_early)
    early_cols = sweep(early_cols, y_a, rim_a, *early_args, y_b, rim_b)
    early_cols = sweep(early_cols, y_b, rim_b, *early_args, y_a, rim_a)

    def keep_early(c, s, new):
        early_out[c, pl.ds(s * CHUNK, CHUNK)] = new

    sweep(early_cols, y_a, rim_a, *early_args, keep_early, None, last=True)

    for c in range(2):
        spread = jnp.where(own_lane == 8 * c, picked(early_out[c]), spread)
    partial = onehot_dot(owner, spread)
    for o in range(n_gx):
        pbuf[o] = partial[o : o + 1]

    for d in range(1, a_count):
        t, device = a_partner(d)
        copy = pltpu.make_async_remote_copy(
            src_ref=pbuf.at[pl.ds(t * per_dev, per_dev)], dst_ref=ra.at[pl.ds(d * per_dev, per_dev)],
            send_sem=a_send.at[d], recv_sem=a_recv, device_id=device, device_id_type=MESH,
        )
        copy.start()
        started.append(copy)
    landed = ra.at[pl.ds(per_dev, n_gx - per_dev)]
    pltpu.make_async_copy(landed, landed, a_recv).wait()
    for r in range(per_dev):
        total = pbuf[q * per_dev + r]
        for d in range(1, a_count):
            total = total + ra[d * per_dev + r]
        sb[r] = total

    pl.semaphore_wait(hello.at[1], len(far))

    def b_copy(r, dest_j):
        dest_i = q * per_dev + r
        own = jnp.logical_and(dest_i == i, j == dest_j)
        return own, pltpu.make_async_remote_copy(
            src_ref=sb.at[r], dst_ref=rb.at[plane], send_sem=b_send.at[r * n_gy + dest_j], recv_sem=b_recv,
            device_id=(dest_i, dest_j), device_id_type=MESH,
        )

    for r in range(per_dev):
        for dest_j in range(n_gy):
            own, copy = b_copy(r, dest_j)
            pl.when(jnp.logical_not(own))(copy.start)
            pl.when(own)(pltpu.make_async_copy(sb.at[r], rb.at[plane], b_recv).start)
    pltpu.make_async_copy(rb, rb, b_recv).wait()
    total = rb[0]
    for p in range(1, planes):
        total = total + rb[p]
    total = jnp.broadcast_to(total, (8, 128))
    out = total
    for k in range(1, 4):
        out = jnp.where(sub1 == k, pltpu.roll(total, 128 - 8 * k, 1), out)
    wells_out[...] = out[0:4, 0:8]

    for copy in started:
        copy.wait_send()
    for r in range(per_dev):
        for dest_j in range(n_gy):
            own, copy = b_copy(r, dest_j)
            pl.when(jnp.logical_not(own))(copy.wait_send)


def per_device(n_gx, n_gy, *args):
    nz = args[5].shape[0]
    a_count = 4 * n_gy
    per_dev = n_gx // a_count
    planes = n_gx // 4
    packs = nz // PACK

    def f32(*lead):
        return pltpu.VMEM((*lead, 8, 128), F32)

    def bf16(*lead):
        return pltpu.VMEM((*lead, 16, 128), BF16)

    dma = pltpu.SemaphoreType.DMA
    vmem = pl.BlockSpec(memory_space=pltpu.VMEM)
    return pl.pallas_call(
        functools.partial(kernel, n_gx, n_gy, nz),
        out_shape=(
            jax.ShapeDtypeStruct((2, nz, 8, 128), F32),
            jax.ShapeDtypeStruct((4, 8), F32),
        ),
        in_specs=[pl.BlockSpec(memory_space=pltpu.HBM)] * 11,
        out_specs=(vmem, vmem),
        scratch_shapes=[pltpu.VMEM(a.shape, a.dtype) for a in args] + [
            dma((11,)),
            f32(2, nz), f32(2, nz), f32(2, nz), f32(2, nz), f32(2, nz + 1),
            f32(2, 4, nz), f32(2, 4, nz), f32(4, nz), f32(2, 2, nz), f32(2, 2, nz),
            f32(2, 2, nz + 2), f32(2, 2, nz + 2),
            f32(6, 2), f32(2, 4), f32(2, 4), f32(2, 2), f32(2, 2), f32(2, 2), f32(2, 2),
            bf16(2, 11, packs), f32(2, 2, 2 * packs), bf16(2, 4, packs), f32(2, 2, 2 * packs),
            bf16(2, 11, packs), f32(2, 2, 2 * packs), bf16(2, 4, packs), f32(2, 2, 2 * packs),
            dma((4, 2)), dma((4, 2)),
            bf16(6), f32(2), bf16(2), f32(2),
            bf16(6, 6), f32(6, 2), bf16(6, 2), f32(6, 2),
            dma((4, 6)), dma((4, 6)),
            pltpu.VMEM((256, 256), BF16), pltpu.VMEM((256, 128), F32),
            pltpu.VMEM((n_gx, 1, 128), F32), pltpu.VMEM((n_gx, 1, 128), F32),
            pltpu.VMEM((per_dev, 1, 128), F32), pltpu.VMEM((planes, 1, 128), F32),
            dma((a_count,)), dma, dma((per_dev * n_gy,)), dma,
            pltpu.SemaphoreType.REGULAR((2,)),
        ],
        compiler_params=pltpu.CompilerParams(
            collective_id=0, has_side_effects=True, vmem_limit_bytes=60 * 1024 * 1024
        ),
    )(*args)


def solution(mesh):
    n_gx, n_gy = mesh.shape["gx"], mesh.shape["gy"]
    cells = P(None, None, "gx", "gy")
    faces = P(None, "gx", "gy")
    perfs = P("gx", "gy", None)
    return jax.shard_map(
        functools.partial(per_device, n_gx, n_gy),
        mesh=mesh,
        in_specs=(cells,) * 5 + (faces,) * 3 + (perfs,) * 3,
        out_specs=(cells, P(None, "gx")),
        check_vma=False,
    )
```

```python
import functools

import jax
import jax.numpy as jnp
from jax import lax
from jax.experimental import pallas as pl
from jax.experimental.pallas import tpu as pltpu
from jax.sharding import PartitionSpec as P

MESH = pl.DeviceIdType.MESH
F32 = jnp.float32
BF16 = jnp.bfloat16
PACK = 4
CHUNK = 2
WIDE = 6


def iota(shape, dim):
    return lax.broadcasted_iota(jnp.int32, shape, dim)


def onehot_dot(onehot, x):
    high = x.astype(BF16)
    low = (x - high.astype(F32)).astype(BF16)
    return jnp.dot(onehot, high, preferred_element_type=F32) + jnp.dot(
        onehot, low, preferred_element_type=F32
    )


def sub_of(x):
    return iota(x.shape, x.ndim - 2)


def row_shift(a, b, amount):
    ra, rb = pltpu.roll(a, amount, a.ndim - 2), pltpu.roll(b, amount, b.ndim - 2)
    edge = sub_of(a) == (0 if amount == 1 else 7)
    return jnp.where(edge, rb, ra), jnp.where(edge, ra, rb)


def pack_rows(x):
    x = x.reshape(x.shape[0] // 2, 2, 8, 128)
    even, odd = x[:, 0], pltpu.roll(x[:, 1], 4, 1)
    first = sub_of(even) < 4
    return jnp.where(first, odd, even), jnp.where(first, even, odd)


def unpack_rows(low, high):
    first = sub_of(low) < 4
    even = jnp.where(first, high, low)
    odd = pltpu.roll(jnp.where(first, low, high), 4, 1)
    return jnp.stack([even, odd], 1).reshape(2 * low.shape[0], 8, 128)


def block_system(accum, mob, faces, live=None):
    d = [accum[k] + faces * mob[k] for k in range(4)]
    det = d[0] * d[3] - d[1] * d[2]
    if live is not None:
        det = jnp.where(live, det, 1.0)
    scale = 1.0 / det
    inv = [d[3] * scale, -d[1] * scale, -d[2] * scale, d[0] * scale]
    b = mob
    mat = [
        inv[0] * b[0] + inv[2] * b[1],
        inv[0] * b[2] + inv[2] * b[3],
        inv[1] * b[0] + inv[3] * b[1],
        inv[1] * b[2] + inv[3] * b[3],
    ]
    return inv, mat


def transpose_apply(m, v):
    return [m[0] * v[0] + m[2] * v[1], m[1] * v[0] + m[3] * v[1]]


def kernel(n_gx, n_gy, nz, *refs):
    inputs, (early_out, wells_out), held = refs[:11], refs[11:13], refs[13:24]
    (
        in_sem, tx, txp, ty, typ, tz, k_late, k_early, inv_early, base_late, base_early, y_a, y_b,
        rim_faces, rim_k_late, rim_k_early, rim_late, rim_early, rim_a, rim_b,
        xs_bf, xs_f, xs_me, xs_e, xr_bf, xr_f, xr_me, xr_e, x_send, x_recv,
        ys_bf, ys_f, ys_me, ys_e, yr_bf, yr_f, yr_me, yr_e, y_send, y_recv,
        cell_row, col_weight, pbuf, ra, sb, rb, a_send, a_recv, b_send, b_recv, hello,
    ) = refs[24:]
    (
        grad_late, grad_early, accum, mob_late, mob_early, trans_x, trans_y, trans_z,
        perf_cell, perf_well, productivity,
    ) = held
    i = lax.axis_index("gx")
    j = lax.axis_index("gy")
    group = 4
    a_count = group * n_gy
    per_dev = n_gx // a_count
    planes = n_gx // group
    plane, spot = i // group, i % group
    q = spot * n_gy + j
    lower, upper = (i + n_gx - 1) % n_gx, (i + 1) % n_gx
    left, right = (j + n_gy - 1) % n_gy, (j + 1) % n_gy
    row_peers = ((upper, j), (lower, j))
    col_peers = ((i, right), (i, left), (lower, right), (lower, left), (upper, right), (upper, left))

    def a_partner(d):
        t = (q + d) % a_count
        return t, (plane * group + t // n_gy, t % n_gy)

    loads = [
        pltpu.make_async_copy(inputs[k], held[k], in_sem.at[k])
        for k in (5, 6, 7, 3, 2, 0, 4, 1, 8, 9, 10)
    ]
    for load in loads:
        load.start()

    def mate(distance):
        return ((i + group * distance + n_gx) % n_gx, j)

    near = [mate(d) for d in (-3, -2, -1, 1, 2, 3)]
    far = [mate(d) for d in (-5, 5)]
    barrier = pltpu.get_barrier_semaphore()
    greeted = [*row_peers, *col_peers, *near] + [a_partner(d)[1] for d in range(1, a_count)]
    for device in greeted:
        pl.semaphore_signal(barrier, inc=1, device_id=device, device_id_type=MESH)
    for load in loads:
        load.wait()

    zero = jnp.zeros((8, 128), F32)
    lane1 = iota((8, 128), 1)
    sub1 = iota((8, 128), 0)
    layer_of = lane1 // WIDE
    col_of = lane1 % WIDE
    live = lane1 < WIDE * nz
    packs = nz // PACK
    steps = nz // CHUNK
    first_row = jnp.where(i == 0, 0, -1)
    first_col = jnp.where(j == 0, 0, -1)

    def pack_cols(old, x, layer, extra=3):
        return jnp.where(layer_of == layer, pltpu.roll(x, extra + WIDE * layer, 1), old)

    def put_rows(x, s, send, k):
        last, first = pack_rows(x)
        if send.dtype == BF16:
            send[0, k, s] = last.reshape(4 * PACK, 128).astype(BF16)
            send[1, k, s] = first.reshape(4 * PACK, 128).astype(BF16)
        else:
            send[0, k, pl.ds(2 * s, 2)] = last
            send[1, k, pl.ds(2 * s, 2)] = first

    def first_out(s, cols):
        at = pl.ds(s * PACK, PACK)
        row, col = iota((PACK, 8, 128), 1), iota((PACK, 8, 128), 2)
        fx = jnp.where(row == first_row, 0.0, trans_x[at].astype(F32))
        fy = jnp.where(col == first_col, 0.0, trans_y[at].astype(F32))
        fz = jnp.where(iota((PACK, 8, 128), 0) + s * PACK == 0, 0.0, trans_z[at].astype(F32))
        tx[0, at] = fx
        ty[0, at] = fy
        tz[0, at] = fz
        fields = [mob_late[k, at].astype(F32) for k in range(4)]
        fields += [accum[k, at].astype(F32) for k in range(4)] + [fx, fy, fz]
        for k, x in enumerate(fields):
            put_rows(x, s, xs_bf, k)
        grads = [grad_late[c, at] for c in range(2)]
        for k, x in enumerate(grads):
            put_rows(x, s, xs_f, k)
        early = [mob_early[k, at].astype(F32) for k in range(4)]
        for k, x in enumerate(early):
            put_rows(x, s, xs_me, k)
        cols = list(cols)
        for t in range(PACK):
            layer = s * PACK + t
            for k, x in enumerate(fields + [fy] + grads + early):
                cols[k] = pack_cols(cols[k], x[t], layer, 2 if k == 11 else 3)
        return tuple(cols)

    cols = lax.fori_loop(0, packs, first_out, (zero,) * 18, unroll=5)
    for k in range(6):
        ys_bf[k] = jnp.concatenate([cols[2 * k], cols[2 * k + 1]], 0).astype(BF16)
    for k in range(2):
        ys_f[k] = cols[12 + k]
        ys_me[k] = jnp.concatenate([cols[14 + 2 * k], cols[15 + 2 * k]], 0).astype(BF16)

    pl.semaphore_wait(barrier, len(greeted))

    started = []

    def send(kind, x_src, x_dst, y_src, y_dst):
        copies = []
        for k, device in enumerate(row_peers):
            copies.append(pltpu.make_async_remote_copy(
                src_ref=x_src.at[k], dst_ref=x_dst.at[k], send_sem=x_send.at[kind, k],
                recv_sem=x_recv.at[kind, k], device_id=device, device_id_type=MESH,
            ))
        for k, device in enumerate(col_peers):
            copies.append(pltpu.make_async_remote_copy(
                src_ref=y_src, dst_ref=y_dst.at[k], send_sem=y_send.at[kind, k],
                recv_sem=y_recv.at[kind, k], device_id=device, device_id_type=MESH,
            ))
        for copy in copies:
            copy.start()
        started.extend(copies)
        return copies

    def arrived(copies):
        for copy in copies:
            copy.wait_recv()

    sent_bf = send(0, xs_bf, xr_bf, ys_bf, yr_bf)
    sent_f = send(1, xs_f, xr_f, ys_f, yr_f)
    sent_me = send(2, xs_me, xr_me, ys_me, yr_me)

    for device in near:
        pl.semaphore_signal(hello.at[0], inc=1, device_id=device, device_id_type=MESH)

    cells = jnp.transpose(jnp.broadcast_to(perf_cell[0], (128, 256)))
    wells = jnp.transpose(jnp.broadcast_to(perf_well[0], (128, 256)))
    prods = jnp.transpose(jnp.broadcast_to(productivity[0], (128, 256)))
    lane_p = iota((256, 128), 1)
    cell_line = cells // 128
    cell_row[:, 0:128] = jnp.where(cell_line == lane_p, 1.0, 0.0).astype(BF16)
    cell_row[:, 128:256] = jnp.where(cell_line == lane_p + 128, 1.0, 0.0).astype(BF16)
    col_weight[...] = jnp.where(cells % 128 == lane_p, prods, 0.0)
    for block in range(2):
        tz[block, nz] = zero
        for buf in (y_a, y_b):
            for c in range(2):
                buf[block, c, 0] = zero
                buf[block, c, nz + 1] = zero

    def get_rows(recv, k, s):
        if recv.dtype == BF16:
            low, high = (recv[d, k, s].astype(F32).reshape(2, 8, 128) for d in range(2))
        else:
            low, high = (recv[d, k, pl.ds(2 * s, 2)] for d in range(2))
        return unpack_rows(low, high)

    def rim(recv, k):
        if recv.dtype == BF16:
            part = [recv[d, k // 2, 0:16].astype(F32)[8 * (k % 2) : 8 * (k % 2) + 8] for d in range(6)]
        else:
            part = [recv[d, k] for d in range(6)]
        beside, up, down = (jnp.where(col_of < 3, part[d], part[d + 1]) for d in (0, 2, 4))
        return beside, jnp.where(sub1 < 4, up, down)

    arrived(sent_bf)

    def rim_trans(s, old):
        at = pl.ds(s * PACK, PACK)
        tx[1, at] = get_rows(xr_bf, 8, s)
        fy = get_rows(xr_bf, 9, s)
        ty[1, at] = fy
        tz[1, at] = get_rows(xr_bf, 10, s)
        for t in range(PACK):
            old = pack_cols(old, fy[t], s * PACK + t)
        return old

    ty_cols = (cols[9], lax.fori_loop(0, packs, rim_trans, zero, unroll=5))
    rim_tx, rim_ty, rim_tz, rim_typ = (rim(yr_bf, k) for k in (8, 9, 10, 11))
    rim_txp = row_shift(*rim_tx, 7)
    rim_all = []
    for block in range(2):
        at_edge = pltpu.roll(ty_cols[block], 127, 1)
        faces = [
            rim_tx[block], rim_txp[block], rim_ty[block],
            jnp.where(col_of == 2, at_edge, rim_typ[block]),
            rim_tz[block], pltpu.roll(rim_tz[block], 128 - WIDE, 1),
        ]
        for k in range(6):
            rim_faces[k, block] = faces[k]
        rim_all.append(faces[0] + faces[1] + faces[2] + faces[3] + faces[4] + faces[5])

    def ends(packed, s):
        return jnp.stack([pltpu.roll(packed, 125 - WIDE * (s * CHUNK + t), 1) for t in range(CHUNK)])

    def faces_late(s, cols):
        cols = [list(c) for c in cols]
        at4 = pl.ds(s * PACK, PACK)
        rim_mob = [get_rows(xr_bf, k, s) for k in range(4)]
        rim_acc = [get_rows(xr_bf, 4 + k, s) for k in range(4)]
        rim_grad = [get_rows(xr_f, c, s) for c in range(2)]
        for h in range(PACK // CHUNK):
            part = slice(h * CHUNK, (h + 1) * CHUNK)
            step = s * (PACK // CHUNK) + h
            at = pl.ds(step * CHUNK, CHUNK)
            after = pl.ds(step * CHUNK + 1, CHUNK)
            lane = iota((CHUNK, 8, 128), 2)
            far_x = row_shift(tx[0, at], tx[1, at], 7)
            for block in range(2):
                fy = ty[block, at]
                far_y = pltpu.roll(jnp.where(lane == 0, ends(rim_ty[block], step), fy), 127, 2)
                txp[block, at] = far_x[block]
                typ[block, at] = far_y
                faces = tx[block, at] + far_x[block] + fy + far_y + tz[block, at] + tz[block, after]
                if block == 0:
                    mob = [mob_late[k, at].astype(F32) for k in range(4)]
                    acc = [accum[k, at].astype(F32) for k in range(4)]
                    grad = [grad_late[c, at] for c in range(2)]
                else:
                    mob, acc, grad = ([x[part] for x in f] for f in (rim_mob, rim_acc, rim_grad))
                inv, mat = block_system(acc, mob, faces)
                for k in range(4):
                    k_late[block, k, at] = mat[k]
                first = transpose_apply(inv, grad)
                for c in range(2):
                    base_late[block, c, at] = first[c]
                    y_a[block, c, after] = first[c]
                    for t in range(CHUNK):
                        cols[block][c] = pack_cols(cols[block][c], first[c][t], step * CHUNK + t)
                if block == 0:
                    mob = [mob_early[k, at].astype(F32) for k in range(4)]
                    inv, mat = block_system(acc, mob, faces)
                    for k in range(4):
                        k_early[0, k, at] = mat[k]
                        inv_early[k, at] = inv[k]
        return tuple(tuple(c) for c in cols)

    arrived(sent_f)
    cols_none = ((zero, zero), (zero, zero))
    late_cols = lax.fori_loop(0, packs, faces_late, cols_none, unroll=5)
    rim_acc_y = [rim(yr_bf, 4 + k) for k in range(4)]
    rim_mob_y = [rim(yr_bf, k) for k in range(4)]
    rim_grad_y = [rim(yr_f, c) for c in range(2)]
    for block in range(2):
        inv, mat = block_system(
            [x[block] for x in rim_acc_y], [x[block] for x in rim_mob_y], rim_all[block], live
        )
        first = transpose_apply(inv, [x[block] for x in rim_grad_y])
        for k in range(4):
            rim_k_late[block, k] = mat[k]
        for c in range(2):
            rim_late[block, c] = first[c]
            rim_a[block, c] = first[c]

    def sweep(cols, y, rim_y, mats, base, rim_mats, rim_base, y_out, rim_out, last=False):
        old = [[rim_y[block, c] for c in range(2)] for block in range(2)]
        blocks = (0,) if last else (0, 1)

        def body(s, packed):
            packed = [list(p) for p in packed]
            at = pl.ds(s * CHUNK, CHUNK)
            at1 = pl.ds(s * CHUNK + 1, CHUNK)
            at2 = pl.ds(s * CHUNK + 2, CHUNK)
            lane = iota((CHUNK, 8, 128), 2)
            flow = [[], []]
            for c in range(2):
                mid = [y[block, c, at1] for block in range(2)]
                below = row_shift(*mid, 1)
                above = row_shift(*mid, 7)
                for block in blocks:
                    side = ends(old[block][c], s)
                    y_low = pltpu.roll(jnp.where(lane == 127, side, mid[block]), 1, 2)
                    y_high = pltpu.roll(jnp.where(lane == 0, side, mid[block]), 127, 2)
                    flow[block].append(
                        tx[block, at] * below[block] + txp[block, at] * above[block]
                        + ty[block, at] * y_low + typ[block, at] * y_high
                        + tz[block, at] * y[block, c, at] + tz[block, at1] * y[block, c, at2]
                    )
            for block in blocks:
                for c in range(2):
                    new = (
                        base[block, c, at] + mats[block, 2 * c, at] * flow[block][0]
                        + mats[block, 2 * c + 1, at] * flow[block][1]
                    )
                    if last:
                        y_out(c, s, new)
                    else:
                        y_out[block, c, at1] = new
                        for t in range(CHUNK):
                            packed[block][c] = pack_cols(packed[block][c], new[t], s * CHUNK + t)
            return tuple(tuple(p) for p in packed)

        packed = lax.fori_loop(0, steps, body, cols_none, unroll=5)
        if last:
            return None
        flow = [[], []]
        for c in range(2):
            below = row_shift(old[0][c], old[1][c], 1)
            above = row_shift(old[0][c], old[1][c], 7)
            for block in range(2):
                mid, own = old[block][c], cols[block][c]
                f = [rim_faces[k, block] for k in range(6)]
                flow[block].append(
                    f[0] * below[block] + f[1] * above[block]
                    + f[2] * pltpu.roll(jnp.where(col_of == 2, own, mid), 1, 1)
                    + f[3] * pltpu.roll(jnp.where(col_of == 3, own, mid), 127, 1)
                    + f[4] * pltpu.roll(mid, WIDE, 1) + f[5] * pltpu.roll(mid, 128 - WIDE, 1)
                )
        for block in range(2):
            for c in range(2):
                rim_out[block, c] = (
                    rim_base[block, c] + rim_mats[block, 2 * c] * flow[block][0]
                    + rim_mats[block, 2 * c + 1] * flow[block][1]
                )
        return packed

    late_args = (k_late, base_late, rim_k_late, rim_late)
    late_cols = sweep(late_cols, y_a, rim_a, *late_args, y_b, rim_b)
    late_cols = sweep(late_cols, y_b, rim_b, *late_args, y_a, rim_a)

    def keep_late(c, s, new):
        y_b[0, c, pl.ds(s * CHUNK + 1, CHUNK)] = new

    sweep(late_cols, y_a, rim_a, *late_args, keep_late, None, last=True)

    def start_early(s, cols):
        cols = list(cols)
        at = pl.ds(s * PACK, PACK)
        at1 = pl.ds(s * PACK + 1, PACK)
        late = [y_b[0, c, at1] for c in range(2)]
        more = transpose_apply([accum[k, at].astype(F32) for k in range(4)], late)
        source = [grad_early[c, at] + more[c] for c in range(2)]
        first = transpose_apply([inv_early[k, at] for k in range(4)], source)
        for c in range(2):
            base_early[0, c, at] = first[c]
            y_a[0, c, at1] = first[c]
            put_rows(first[c], s, xs_e, c)
            for t in range(PACK):
                cols[c] = pack_cols(cols[c], first[c][t], s * PACK + t)
        return tuple(cols)

    own_cols = lax.fori_loop(0, packs, start_early, (zero, zero), unroll=5)
    for c in range(2):
        ys_e[c] = own_cols[c]
    sent_e = send(3, xs_e, xr_e, ys_e, yr_e)

    pl.semaphore_wait(hello.at[0], len(near))
    for device in far:
        pl.semaphore_signal(hello.at[1], inc=1, device_id=device, device_id_type=MESH)
    arrived(sent_me)

    def rim_early_mats(s, _):
        rim_mob = [get_rows(xr_me, k, s) for k in range(4)]
        rim_acc = [get_rows(xr_bf, 4 + k, s) for k in range(4)]
        at = pl.ds(s * PACK, PACK)
        after = pl.ds(s * PACK + 1, PACK)
        faces = tx[1, at] + txp[1, at] + ty[1, at] + typ[1, at] + tz[1, at] + tz[1, after]
        _, mat = block_system(rim_acc, rim_mob, faces)
        for k in range(4):
            k_early[1, k, at] = mat[k]
        return 0

    lax.fori_loop(0, packs, rim_early_mats, 0, unroll=5)
    rim_mob_y = [rim(yr_me, k) for k in range(4)]
    for block in range(2):
        _, mat = block_system(
            [x[block] for x in rim_acc_y], [x[block] for x in rim_mob_y], rim_all[block], live
        )
        for k in range(4):
            rim_k_early[block, k] = mat[k]

    pad = jnp.zeros((256 - 8 * nz, 128), F32)

    def picked(field):
        lines = jnp.concatenate([field.reshape(8 * nz, 128), pad], 0)
        terms = onehot_dot(cell_row[...], lines) * col_weight[...]
        return jnp.sum(terms, axis=1, keepdims=True)

    own_lane = lane_p - wells % 8
    spread = jnp.zeros((256, 128), F32)
    for c in range(2):
        spread = jnp.where(own_lane == 8 * (c + 2), picked(y_b[0, c, pl.ds(1, nz)]), spread)
    owner = jnp.where(
        iota((n_gx, 256), 0) == jnp.broadcast_to(perf_well[0] // 8, (n_gx, 256)), 1.0, 0.0
    ).astype(BF16)

    arrived(sent_e)

    def rim_start(s, cols):
        cols = list(cols)
        at = pl.ds(s * PACK, PACK)
        at1 = pl.ds(s * PACK + 1, PACK)
        for c in range(2):
            first = get_rows(xr_e, c, s)
            base_early[1, c, at] = first
            y_a[1, c, at1] = first
            for t in range(PACK):
                cols[c] = pack_cols(cols[c], first[t], s * PACK + t)
        return tuple(cols)

    early_cols = (own_cols, lax.fori_loop(0, packs, rim_start, (zero, zero), unroll=5))
    for c in range(2):
        pair = rim(yr_e, c)
        for block in range(2):
            rim_early[block, c] = pair[block]
            rim_a[block, c] = pair[block]

    early_args = (k_early, base_early, rim_k_early, rim_early)
    early_cols = sweep(early_cols, y_a, rim_a, *early_args, y_b, rim_b)
    early_cols = sweep(early_cols, y_b, rim_b, *early_args, y_a, rim_a)

    def keep_early(c, s, new):
        early_out[c, pl.ds(s * CHUNK, CHUNK)] = new

    sweep(early_cols, y_a, rim_a, *early_args, keep_early, None, last=True)

    for c in range(2):
        spread = jnp.where(own_lane == 8 * c, picked(early_out[c]), spread)
    partial = onehot_dot(owner, spread)
    for o in range(n_gx):
        pbuf[o] = partial[o : o + 1]

    for d in range(1, a_count):
        t, device = a_partner(d)
        copy = pltpu.make_async_remote_copy(
            src_ref=pbuf.at[pl.ds(t * per_dev, per_dev)], dst_ref=ra.at[pl.ds(d * per_dev, per_dev)],
            send_sem=a_send.at[d], recv_sem=a_recv, device_id=device, device_id_type=MESH,
        )
        copy.start()
        started.append(copy)
    landed = ra.at[pl.ds(per_dev, n_gx - per_dev)]
    pltpu.make_async_copy(landed, landed, a_recv).wait()
    for r in range(per_dev):
        total = pbuf[q * per_dev + r]
        for d in range(1, a_count):
            total = total + ra[d * per_dev + r]
        sb[r] = total

    pl.semaphore_wait(hello.at[1], len(far))

    def b_copy(r, dest_j):
        dest_i = q * per_dev + r
        own = jnp.logical_and(dest_i == i, j == dest_j)
        return own, pltpu.make_async_remote_copy(
            src_ref=sb.at[r], dst_ref=rb.at[plane], send_sem=b_send.at[r * n_gy + dest_j], recv_sem=b_recv,
            device_id=(dest_i, dest_j), device_id_type=MESH,
        )

    for r in range(per_dev):
        for dest_j in range(n_gy):
            own, copy = b_copy(r, dest_j)
            pl.when(jnp.logical_not(own))(copy.start)
            pl.when(own)(pltpu.make_async_copy(sb.at[r], rb.at[plane], b_recv).start)
    pltpu.make_async_copy(rb, rb, b_recv).wait()
    total = rb[0]
    for p in range(1, planes):
        total = total + rb[p]
    total = jnp.broadcast_to(total, (8, 128))
    out = total
    for k in range(1, 4):
        out = jnp.where(sub1 == k, pltpu.roll(total, 128 - 8 * k, 1), out)
    wells_out[...] = out[0:4, 0:8]

    for copy in started:
        copy.wait_send()
    for r in range(per_dev):
        for dest_j in range(n_gy):
            own, copy = b_copy(r, dest_j)
            pl.when(jnp.logical_not(own))(copy.wait_send)


def per_device(n_gx, n_gy, *args):
    nz = args[5].shape[0]
    a_count = 4 * n_gy
    per_dev = n_gx // a_count
    planes = n_gx // 4
    packs = nz // PACK

    def f32(*lead):
        return pltpu.VMEM((*lead, 8, 128), F32)

    def bf16(*lead):
        return pltpu.VMEM((*lead, 16, 128), BF16)

    dma = pltpu.SemaphoreType.DMA
    vmem = pl.BlockSpec(memory_space=pltpu.VMEM)
    return pl.pallas_call(
        functools.partial(kernel, n_gx, n_gy, nz),
        out_shape=(
            jax.ShapeDtypeStruct((2, nz, 8, 128), F32),
            jax.ShapeDtypeStruct((4, 8), F32),
        ),
        in_specs=[pl.BlockSpec(memory_space=pltpu.HBM)] * 11,
        out_specs=(vmem, vmem),
        scratch_shapes=[pltpu.VMEM(a.shape, a.dtype) for a in args] + [
            dma((11,)),
            f32(2, nz), f32(2, nz), f32(2, nz), f32(2, nz), f32(2, nz + 1),
            f32(2, 4, nz), f32(2, 4, nz), f32(4, nz), f32(2, 2, nz), f32(2, 2, nz),
            f32(2, 2, nz + 2), f32(2, 2, nz + 2),
            f32(6, 2), f32(2, 4), f32(2, 4), f32(2, 2), f32(2, 2), f32(2, 2), f32(2, 2),
            bf16(2, 11, packs), f32(2, 2, 2 * packs), bf16(2, 4, packs), f32(2, 2, 2 * packs),
            bf16(2, 11, packs), f32(2, 2, 2 * packs), bf16(2, 4, packs), f32(2, 2, 2 * packs),
            dma((4, 2)), dma((4, 2)),
            bf16(6), f32(2), bf16(2), f32(2),
            bf16(6, 6), f32(6, 2), bf16(6, 2), f32(6, 2),
            dma((4, 6)), dma((4, 6)),
            pltpu.VMEM((256, 256), BF16), pltpu.VMEM((256, 128), F32),
            pltpu.VMEM((n_gx, 1, 128), F32), pltpu.VMEM((n_gx, 1, 128), F32),
            pltpu.VMEM((per_dev, 1, 128), F32), pltpu.VMEM((planes, 1, 128), F32),
            dma((a_count,)), dma, dma((per_dev * n_gy,)), dma,
            pltpu.SemaphoreType.REGULAR((2,)),
        ],
        compiler_params=pltpu.CompilerParams(
            collective_id=0, has_side_effects=True, vmem_limit_bytes=60 * 1024 * 1024
        ),
    )(*args)


def solution(mesh):
    n_gx, n_gy = mesh.shape["gx"], mesh.shape["gy"]
    cells = P(None, None, "gx", "gy")
    faces = P(None, "gx", "gy")
    perfs = P("gx", "gy", None)
    return jax.shard_map(
        functools.partial(per_device, n_gx, n_gy),
        mesh=mesh,
        in_specs=(cells,) * 5 + (faces,) * 3 + (perfs,) * 3,
        out_specs=(cells, P(None, "gx")),
        check_vma=False,
    )
```

```python
import functools

import jax
import jax.numpy as jnp
from jax import lax
from jax.experimental import pallas as pl
from jax.experimental.pallas import tpu as pltpu
from jax.sharding import PartitionSpec as P

MESH = pl.DeviceIdType.MESH
F32 = jnp.float32
BF16 = jnp.bfloat16
PACK = 4
CHUNK = 2
WIDE = 6


def iota(shape, dim):
    return lax.broadcasted_iota(jnp.int32, shape, dim)


def onehot_dot(onehot, x):
    high = x.astype(BF16)
    low = (x - high.astype(F32)).astype(BF16)
    return jnp.dot(onehot, high, preferred_element_type=F32) + jnp.dot(
        onehot, low, preferred_element_type=F32
    )


def sub_of(x):
    return iota(x.shape, x.ndim - 2)


def row_shift(a, b, amount):
    ra, rb = pltpu.roll(a, amount, a.ndim - 2), pltpu.roll(b, amount, b.ndim - 2)
    edge = sub_of(a) == (0 if amount == 1 else 7)
    return jnp.where(edge, rb, ra), jnp.where(edge, ra, rb)


def pack_rows(x):
    x = x.reshape(x.shape[0] // 2, 2, 8, 128)
    even, odd = x[:, 0], pltpu.roll(x[:, 1], 4, 1)
    first = sub_of(even) < 4
    return jnp.where(first, odd, even), jnp.where(first, even, odd)


def unpack_rows(low, high):
    first = sub_of(low) < 4
    even = jnp.where(first, high, low)
    odd = pltpu.roll(jnp.where(first, low, high), 4, 1)
    return jnp.stack([even, odd], 1).reshape(2 * low.shape[0], 8, 128)


def block_system(accum, mob, faces, live=None):
    d = [accum[k] + faces * mob[k] for k in range(4)]
    det = d[0] * d[3] - d[1] * d[2]
    if live is not None:
        det = jnp.where(live, det, 1.0)
    scale = 1.0 / det
    inv = [d[3] * scale, -d[1] * scale, -d[2] * scale, d[0] * scale]
    b = mob
    mat = [
        inv[0] * b[0] + inv[2] * b[1],
        inv[0] * b[2] + inv[2] * b[3],
        inv[1] * b[0] + inv[3] * b[1],
        inv[1] * b[2] + inv[3] * b[3],
    ]
    return inv, mat


def transpose_apply(m, v):
    return [m[0] * v[0] + m[2] * v[1], m[1] * v[0] + m[3] * v[1]]


def kernel(n_gx, n_gy, nz, *refs):
    inputs, (early_out, wells_out), held = refs[:11], refs[11:13], refs[13:24]
    (
        in_sem, tx, txp, ty, typ, tz, k_late, k_early, inv_early, base_late, base_early, y_a, y_b,
        rim_faces, rim_k_late, rim_k_early, rim_late, rim_early, rim_a, rim_b,
        xs_bf, xs_f, xs_me, xs_e, xr_bf, xr_f, xr_me, xr_e, x_send, x_recv,
        ys_bf, ys_f, ys_me, ys_e, yr_bf, yr_f, yr_me, yr_e, y_send, y_recv,
        zs_bf, zs_f, zs_e, zr_bf, zr_f, zr_e, z_send, z_recv,
        cell_row, col_weight, pbuf, ra, sb, rb, a_send, a_recv, b_send, b_recv, hello,
    ) = refs[24:]
    (
        grad_late, grad_early, accum, mob_late, mob_early, trans_x, trans_y, trans_z,
        perf_cell, perf_well, productivity,
    ) = held
    i = lax.axis_index("gx")
    j = lax.axis_index("gy")
    group = 4
    a_count = group * n_gy
    per_dev = n_gx // a_count
    planes = n_gx // group
    plane, spot = i // group, i % group
    q = spot * n_gy + j
    lower, upper = (i + n_gx - 1) % n_gx, (i + 1) % n_gx
    left, right = (j + n_gy - 1) % n_gy, (j + 1) % n_gy
    row_peers = ((upper, j), (lower, j))
    col_peers = ((i, right), (i, left))
    corner_peers = ((upper, right), (upper, left), (lower, right), (lower, left))
    px, py, core = 2 * (j % 2) + spot // 2, j // 2, spot % 2
    offsets = sorted(
        ((dx, dy, dc) for dx in range(4) for dy in range(4) for dc in range(2)),
        key=lambda o: -min(o[0], 4 - o[0]) - min(o[1], 4 - o[1]) - o[2] / 2,
    )

    def a_partner(d):
        dx, dy, dc = offsets[d]
        x, to_core = (px + dx) % 4, core + dc - 2 * core * dc
        to_j, to_spot = ((py + dy) % 4) * 2 + x // 2, (x % 2) * 2 + to_core
        return to_spot * n_gy + to_j, (plane * group + to_spot, to_j)

    loads = [
        pltpu.make_async_copy(inputs[k], held[k], in_sem.at[k])
        for k in (5, 6, 7, 3, 2, 0, 4, 1, 8, 9, 10)
    ]
    for load in loads:
        load.start()

    def mate(distance):
        return ((i + group * distance + n_gx) % n_gx, j)

    near = [mate(d) for d in (-3, -2, -1, 1, 2, 3)]
    far = [mate(d) for d in (-5, 5)]
    barrier = pltpu.get_barrier_semaphore()
    greeted = [*row_peers, *col_peers, *corner_peers, *near] + [a_partner(d)[1] for d in range(a_count - 1)]
    for device in greeted:
        pl.semaphore_signal(barrier, inc=1, device_id=device, device_id_type=MESH)
    for load in loads:
        load.wait()

    zero = jnp.zeros((8, 128), F32)
    lane1 = iota((8, 128), 1)
    sub1 = iota((8, 128), 0)
    layer_of = lane1 // WIDE
    col_of = lane1 % WIDE
    live = lane1 < WIDE * nz
    packs = nz // PACK
    steps = nz // CHUNK
    first_row = jnp.where(i == 0, 0, -1)
    first_col = jnp.where(j == 0, 0, -1)

    def pack_cols(old, x, layer, extra=3):
        return jnp.where(layer_of == layer, pltpu.roll(x, extra + WIDE * layer, 1), old)

    def put_rows(x, s, send, k):
        last, first = pack_rows(x)
        if send.dtype == BF16:
            send[0, k, s] = last.reshape(4 * PACK, 128).astype(BF16)
            send[1, k, s] = first.reshape(4 * PACK, 128).astype(BF16)
        else:
            send[0, k, pl.ds(2 * s, 2)] = last
            send[1, k, pl.ds(2 * s, 2)] = first

    def first_out(s, cols):
        at = pl.ds(s * PACK, PACK)
        row, col = iota((PACK, 8, 128), 1), iota((PACK, 8, 128), 2)
        fx = jnp.where(row == first_row, 0.0, trans_x[at].astype(F32))
        fy = jnp.where(col == first_col, 0.0, trans_y[at].astype(F32))
        fz = jnp.where(iota((PACK, 8, 128), 0) + s * PACK == 0, 0.0, trans_z[at].astype(F32))
        tx[0, at] = fx
        ty[0, at] = fy
        tz[0, at] = fz
        fields = [mob_late[k, at].astype(F32) for k in range(4)]
        fields += [accum[k, at].astype(F32) for k in range(4)] + [fx, fy, fz]
        for k, x in enumerate(fields):
            put_rows(x, s, xs_bf, k)
        grads = [grad_late[c, at] for c in range(2)]
        for k, x in enumerate(grads):
            put_rows(x, s, xs_f, k)
        early = [mob_early[k, at].astype(F32) for k in range(4)]
        for k, x in enumerate(early):
            put_rows(x, s, xs_me, k)
        cols = list(cols)
        for t in range(PACK):
            layer = s * PACK + t
            for k, x in enumerate(fields + [fy] + grads + early):
                cols[k] = pack_cols(cols[k], x[t], layer, 2 if k == 11 else 3)
        return tuple(cols)

    cols = lax.fori_loop(0, packs, first_out, (zero,) * 18, unroll=5)
    def pair_cols(a, b):
        return (
            jnp.where(col_of < 3, a, pltpu.roll(b, 3, 1)),
            jnp.where(col_of < 3, pltpu.roll(a, 125, 1), b),
        )

    def pair_corners(p, r):
        turned = pltpu.roll(r, 4, 0)
        return jnp.where(sub1 < 4, turned, p), jnp.where(sub1 < 4, p, turned)

    def to_bf(a, b):
        return jnp.concatenate([a, b], 0).astype(BF16)

    pairs = [pair_cols(cols[2 * k], cols[2 * k + 1]) for k in range(9)]
    for side in range(2):
        part = [p[side] for p in pairs]
        for k in range(3):
            ys_bf[side, k] = to_bf(part[2 * k], part[2 * k + 1])
        ys_f[side] = part[6]
        ys_me[side] = to_bf(part[7], part[8])
        order = (0, 1, 2, 3, 4, 5, 7, 8)
        quads = [pair_corners(part[order[2 * k]], part[order[2 * k + 1]]) for k in range(4)]
        for end in range(2):
            for k in range(2):
                zs_bf[2 * end + side, k] = to_bf(quads[2 * k][end], quads[2 * k + 1][end])
            zs_f[2 * end + side] = part[6]

    pl.semaphore_wait(barrier, len(greeted))

    started = []

    def send(kind, *parts):
        copies = []
        for src, dst, peers, sems in parts:
            for k, device in enumerate(peers):
                copies.append(pltpu.make_async_remote_copy(
                    src_ref=src.at[k], dst_ref=dst.at[k], send_sem=sems[0].at[kind, k],
                    recv_sem=sems[1].at[kind, k], device_id=device, device_id_type=MESH,
                ))
        for copy in copies:
            copy.start()
        started.extend(copies)
        return copies

    rows = row_peers, (x_send, x_recv)
    sides = col_peers, (y_send, y_recv)
    corners = corner_peers, (z_send, z_recv)

    def arrived(copies):
        for copy in copies:
            copy.wait_recv()

    sent_bf = send(0, (xs_bf, xr_bf, *rows), (zs_bf, zr_bf, *corners), (ys_bf, yr_bf, *sides))
    sent_f = send(1, (xs_f, xr_f, *rows), (zs_f, zr_f, *corners), (ys_f, yr_f, *sides))

    for device in near:
        pl.semaphore_signal(hello.at[0], inc=1, device_id=device, device_id_type=MESH)

    cells = jnp.transpose(jnp.broadcast_to(perf_cell[0], (128, 256)))
    wells = jnp.transpose(jnp.broadcast_to(perf_well[0], (128, 256)))
    prods = jnp.transpose(jnp.broadcast_to(productivity[0], (128, 256)))
    lane_p = iota((256, 128), 1)
    cell_line = cells // 128
    cell_row[:, 0:128] = jnp.where(cell_line == lane_p, 1.0, 0.0).astype(BF16)
    cell_row[:, 128:256] = jnp.where(cell_line == lane_p + 128, 1.0, 0.0).astype(BF16)
    col_weight[...] = jnp.where(cells % 128 == lane_p, prods, 0.0)
    for block in range(2):
        tz[block, nz] = zero
        for buf in (y_a, y_b):
            for c in range(2):
                buf[block, c, 0] = zero
                buf[block, c, nz + 1] = zero

    def get_rows(recv, k, s):
        if recv.dtype == BF16:
            low, high = (recv[d, k, s].astype(F32).reshape(2, 8, 128) for d in range(2))
        else:
            low, high = (recv[d, k, pl.ds(2 * s, 2)] for d in range(2))
        return unpack_rows(low, high)

    def split_cols(a, b):
        return (
            jnp.where(col_of < 3, a, pltpu.roll(b, 3, 1)),
            jnp.where(col_of < 3, pltpu.roll(a, 125, 1), b),
        )

    def halves(tile):
        tile = tile.astype(F32)
        return tile[0:8], tile[8:16]

    def split_rows(down, up):
        return jnp.where(sub1 < 4, up, down), pltpu.roll(jnp.where(sub1 < 4, down, up), 4, 0)

    def rim_fields(y_tiles, z_tiles):
        beside = [split_cols(*pair) for pair in zip(*y_tiles)]
        corner = [split_cols(*pair) for pair in zip(*z_tiles)]
        return [(beside[k // 2][k % 2], corner[k // 2][k % 2]) for k in range(2 * len(beside))]

    def corner_bf(quads):
        tiles = []
        for side in range(2):
            part = []
            for k in quads:
                down, up = (halves(zr_bf[d + side, k // 2])[k % 2] for d in (0, 2))
                part += split_rows(down, up)
            tiles.append(part)
        return tiles

    def corner_f(recv):
        return [[jnp.where(sub1 < 4, recv[2 + side], recv[side])] for side in range(2)]

    arrived(sent_bf)

    def rim_trans(s, old):
        at = pl.ds(s * PACK, PACK)
        tx[1, at] = get_rows(xr_bf, 8, s)
        fy = get_rows(xr_bf, 9, s)
        ty[1, at] = fy
        tz[1, at] = get_rows(xr_bf, 10, s)
        for t in range(PACK):
            old = pack_cols(old, fy[t], s * PACK + t)
        return old

    ty_cols = (cols[9], lax.fori_loop(0, packs, rim_trans, zero, unroll=5))
    rim_bf = rim_fields(
        [[h for k in range(3) for h in halves(yr_bf[side, k])] for side in range(2)],
        corner_bf((0, 1, 2)),
    )
    rim_tx, rim_ty, rim_tz, rim_typ = rim_bf[8:12]
    rim_txp = row_shift(*rim_tx, 7)
    rim_all = []
    for block in range(2):
        at_edge = pltpu.roll(ty_cols[block], 127, 1)
        faces = [
            rim_tx[block], rim_txp[block], rim_ty[block],
            jnp.where(col_of == 2, at_edge, rim_typ[block]),
            rim_tz[block], pltpu.roll(rim_tz[block], 128 - WIDE, 1),
        ]
        for k in range(6):
            rim_faces[k, block] = faces[k]
        rim_all.append(faces[0] + faces[1] + faces[2] + faces[3] + faces[4] + faces[5])

    def ends(packed, s):
        return jnp.stack([pltpu.roll(packed, 125 - WIDE * (s * CHUNK + t), 1) for t in range(CHUNK)])

    def faces_late(s, cols):
        cols = [list(c) for c in cols]
        at4 = pl.ds(s * PACK, PACK)
        rim_mob = [get_rows(xr_bf, k, s) for k in range(4)]
        rim_acc = [get_rows(xr_bf, 4 + k, s) for k in range(4)]
        rim_grad = [get_rows(xr_f, c, s) for c in range(2)]
        for h in range(PACK // CHUNK):
            part = slice(h * CHUNK, (h + 1) * CHUNK)
            step = s * (PACK // CHUNK) + h
            at = pl.ds(step * CHUNK, CHUNK)
            after = pl.ds(step * CHUNK + 1, CHUNK)
            lane = iota((CHUNK, 8, 128), 2)
            far_x = row_shift(tx[0, at], tx[1, at], 7)
            for block in range(2):
                fy = ty[block, at]
                far_y = pltpu.roll(jnp.where(lane == 0, ends(rim_ty[block], step), fy), 127, 2)
                txp[block, at] = far_x[block]
                typ[block, at] = far_y
                faces = tx[block, at] + far_x[block] + fy + far_y + tz[block, at] + tz[block, after]
                if block == 0:
                    mob = [mob_late[k, at].astype(F32) for k in range(4)]
                    acc = [accum[k, at].astype(F32) for k in range(4)]
                    grad = [grad_late[c, at] for c in range(2)]
                else:
                    mob, acc, grad = ([x[part] for x in f] for f in (rim_mob, rim_acc, rim_grad))
                inv, mat = block_system(acc, mob, faces)
                for k in range(4):
                    k_late[block, k, at] = mat[k]
                first = transpose_apply(inv, grad)
                for c in range(2):
                    base_late[block, c, at] = first[c]
                    y_a[block, c, after] = first[c]
                    for t in range(CHUNK):
                        cols[block][c] = pack_cols(cols[block][c], first[c][t], step * CHUNK + t)
                if block == 0:
                    mob = [mob_early[k, at].astype(F32) for k in range(4)]
                    inv, mat = block_system(acc, mob, faces)
                    for k in range(4):
                        k_early[0, k, at] = mat[k]
                        inv_early[k, at] = inv[k]
        return tuple(tuple(c) for c in cols)

    arrived(sent_f)
    sent_me = send(2, (xs_me, xr_me, *rows), (ys_me, yr_me, *sides))
    cols_none = ((zero, zero), (zero, zero))
    late_cols = lax.fori_loop(0, packs, faces_late, cols_none, unroll=5)
    rim_mob_y, rim_acc_y = rim_bf[0:4], rim_bf[4:8]
    rim_grad_y = rim_fields([[yr_f[side]] for side in range(2)], corner_f(zr_f))
    for block in range(2):
        inv, mat = block_system(
            [x[block] for x in rim_acc_y], [x[block] for x in rim_mob_y], rim_all[block], live
        )
        first = transpose_apply(inv, [x[block] for x in rim_grad_y])
        for k in range(4):
            rim_k_late[block, k] = mat[k]
        for c in range(2):
            rim_late[block, c] = first[c]
            rim_a[block, c] = first[c]

    def sweep(cols, y, rim_y, mats, base, rim_mats, rim_base, y_out, rim_out, last=False):
        old = [[rim_y[block, c] for c in range(2)] for block in range(2)]
        blocks = (0,) if last else (0, 1)

        def body(s, packed):
            packed = [list(p) for p in packed]
            at = pl.ds(s * CHUNK, CHUNK)
            at1 = pl.ds(s * CHUNK + 1, CHUNK)
            at2 = pl.ds(s * CHUNK + 2, CHUNK)
            lane = iota((CHUNK, 8, 128), 2)
            flow = [[], []]
            for c in range(2):
                mid = [y[block, c, at1] for block in range(2)]
                below = row_shift(*mid, 1)
                above = row_shift(*mid, 7)
                for block in blocks:
                    side = ends(old[block][c], s)
                    y_low = pltpu.roll(jnp.where(lane == 127, side, mid[block]), 1, 2)
                    y_high = pltpu.roll(jnp.where(lane == 0, side, mid[block]), 127, 2)
                    flow[block].append(
                        tx[block, at] * below[block] + txp[block, at] * above[block]
                        + ty[block, at] * y_low + typ[block, at] * y_high
                        + tz[block, at] * y[block, c, at] + tz[block, at1] * y[block, c, at2]
                    )
            for block in blocks:
                for c in range(2):
                    new = (
                        base[block, c, at] + mats[block, 2 * c, at] * flow[block][0]
                        + mats[block, 2 * c + 1, at] * flow[block][1]
                    )
                    if last:
                        y_out(c, s, new)
                    else:
                        y_out[block, c, at1] = new
                        for t in range(CHUNK):
                            packed[block][c] = pack_cols(packed[block][c], new[t], s * CHUNK + t)
            return tuple(tuple(p) for p in packed)

        packed = lax.fori_loop(0, steps, body, cols_none, unroll=5)
        if last:
            return None
        flow = [[], []]
        for c in range(2):
            below = row_shift(old[0][c], old[1][c], 1)
            above = row_shift(old[0][c], old[1][c], 7)
            for block in range(2):
                mid, own = old[block][c], cols[block][c]
                f = [rim_faces[k, block] for k in range(6)]
                flow[block].append(
                    f[0] * below[block] + f[1] * above[block]
                    + f[2] * pltpu.roll(jnp.where(col_of == 2, own, mid), 1, 1)
                    + f[3] * pltpu.roll(jnp.where(col_of == 3, own, mid), 127, 1)
                    + f[4] * pltpu.roll(mid, WIDE, 1) + f[5] * pltpu.roll(mid, 128 - WIDE, 1)
                )
        for block in range(2):
            for c in range(2):
                rim_out[block, c] = (
                    rim_base[block, c] + rim_mats[block, 2 * c] * flow[block][0]
                    + rim_mats[block, 2 * c + 1] * flow[block][1]
                )
        return packed

    late_args = (k_late, base_late, rim_k_late, rim_late)
    late_cols = sweep(late_cols, y_a, rim_a, *late_args, y_b, rim_b)
    late_cols = sweep(late_cols, y_b, rim_b, *late_args, y_a, rim_a)

    def keep_late(c, s, new):
        y_b[0, c, pl.ds(s * CHUNK + 1, CHUNK)] = new

    sweep(late_cols, y_a, rim_a, *late_args, keep_late, None, last=True)

    def start_early(s, cols):
        cols = list(cols)
        at = pl.ds(s * PACK, PACK)
        at1 = pl.ds(s * PACK + 1, PACK)
        late = [y_b[0, c, at1] for c in range(2)]
        more = transpose_apply([accum[k, at].astype(F32) for k in range(4)], late)
        source = [grad_early[c, at] + more[c] for c in range(2)]
        first = transpose_apply([inv_early[k, at] for k in range(4)], source)
        for c in range(2):
            base_early[0, c, at] = first[c]
            y_a[0, c, at1] = first[c]
            put_rows(first[c], s, xs_e, c)
            for t in range(PACK):
                cols[c] = pack_cols(cols[c], first[c][t], s * PACK + t)
        return tuple(cols)

    own_cols = lax.fori_loop(0, packs, start_early, (zero, zero), unroll=5)
    pair = pair_cols(*own_cols)
    for side in range(2):
        ys_e[side] = pair[side]
        for end in range(2):
            zs_e[2 * end + side] = pair[side]
    sent_e = send(3, (xs_e, xr_e, *rows), (zs_e, zr_e, *corners), (ys_e, yr_e, *sides))

    pl.semaphore_wait(hello.at[0], len(near))
    for device in far:
        pl.semaphore_signal(hello.at[1], inc=1, device_id=device, device_id_type=MESH)
    arrived(sent_me)

    def rim_early_mats(s, _):
        rim_mob = [get_rows(xr_me, k, s) for k in range(4)]
        rim_acc = [get_rows(xr_bf, 4 + k, s) for k in range(4)]
        at = pl.ds(s * PACK, PACK)
        after = pl.ds(s * PACK + 1, PACK)
        faces = tx[1, at] + txp[1, at] + ty[1, at] + typ[1, at] + tz[1, at] + tz[1, after]
        _, mat = block_system(rim_acc, rim_mob, faces)
        for k in range(4):
            k_early[1, k, at] = mat[k]
        return 0

    lax.fori_loop(0, packs, rim_early_mats, 0, unroll=5)
    rim_mob_y = rim_fields([halves(yr_me[side]) for side in range(2)], corner_bf((3,)))
    for block in range(2):
        _, mat = block_system(
            [x[block] for x in rim_acc_y], [x[block] for x in rim_mob_y], rim_all[block], live
        )
        for k in range(4):
            rim_k_early[block, k] = mat[k]

    pad = jnp.zeros((256 - 8 * nz, 128), F32)

    def picked(field):
        lines = jnp.concatenate([field.reshape(8 * nz, 128), pad], 0)
        terms = onehot_dot(cell_row[...], lines) * col_weight[...]
        return jnp.sum(terms, axis=1, keepdims=True)

    own_lane = lane_p - wells % 8
    spread = jnp.zeros((256, 128), F32)
    for c in range(2):
        spread = jnp.where(own_lane == 8 * (c + 2), picked(y_b[0, c, pl.ds(1, nz)]), spread)
    owner = jnp.where(
        iota((n_gx, 256), 0) == jnp.broadcast_to(perf_well[0] // 8, (n_gx, 256)), 1.0, 0.0
    ).astype(BF16)

    arrived(sent_e)

    def rim_start(s, cols):
        cols = list(cols)
        at = pl.ds(s * PACK, PACK)
        at1 = pl.ds(s * PACK + 1, PACK)
        for c in range(2):
            first = get_rows(xr_e, c, s)
            base_early[1, c, at] = first
            y_a[1, c, at1] = first
            for t in range(PACK):
                cols[c] = pack_cols(cols[c], first[t], s * PACK + t)
        return tuple(cols)

    early_cols = (own_cols, lax.fori_loop(0, packs, rim_start, (zero, zero), unroll=5))
    rim_first = rim_fields([[yr_e[side]] for side in range(2)], corner_f(zr_e))
    for c in range(2):
        pair = rim_first[c]
        for block in range(2):
            rim_early[block, c] = pair[block]
            rim_a[block, c] = pair[block]

    early_args = (k_early, base_early, rim_k_early, rim_early)
    early_cols = sweep(early_cols, y_a, rim_a, *early_args, y_b, rim_b)
    early_cols = sweep(early_cols, y_b, rim_b, *early_args, y_a, rim_a)

    def keep_early(c, s, new):
        early_out[c, pl.ds(s * CHUNK, CHUNK)] = new

    sweep(early_cols, y_a, rim_a, *early_args, keep_early, None, last=True)

    for c in range(2):
        spread = jnp.where(own_lane == 8 * c, picked(early_out[c]), spread)
    partial = onehot_dot(owner, spread)
    for o in range(n_gx):
        pbuf[o] = partial[o : o + 1]

    for d in range(a_count - 1):
        t, device = a_partner(d)
        copy = pltpu.make_async_remote_copy(
            src_ref=pbuf.at[pl.ds(t * per_dev, per_dev)], dst_ref=ra.at[pl.ds(d * per_dev, per_dev)],
            send_sem=a_send.at[d], recv_sem=a_recv, device_id=device, device_id_type=MESH,
        )
        copy.start()
        started.append(copy)
    landed = ra.at[pl.ds(0, n_gx - per_dev)]
    pltpu.make_async_copy(landed, landed, a_recv).wait()
    for r in range(per_dev):
        total = pbuf[q * per_dev + r]
        for d in range(a_count - 1):
            total = total + ra[d * per_dev + r]
        sb[r] = total

    pl.semaphore_wait(hello.at[1], len(far))

    def b_copy(r, dest_j):
        dest_i = q * per_dev + r
        own = jnp.logical_and(dest_i == i, j == dest_j)
        return own, pltpu.make_async_remote_copy(
            src_ref=sb.at[r], dst_ref=rb.at[plane], send_sem=b_send.at[r * n_gy + dest_j], recv_sem=b_recv,
            device_id=(dest_i, dest_j), device_id_type=MESH,
        )

    for r in range(per_dev):
        for dest_j in range(n_gy):
            own, copy = b_copy(r, dest_j)
            pl.when(jnp.logical_not(own))(copy.start)
            pl.when(own)(pltpu.make_async_copy(sb.at[r], rb.at[plane], b_recv).start)
    pltpu.make_async_copy(rb, rb, b_recv).wait()
    total = rb[0]
    for p in range(1, planes):
        total = total + rb[p]
    total = jnp.broadcast_to(total, (8, 128))
    out = total
    for k in range(1, 4):
        out = jnp.where(sub1 == k, pltpu.roll(total, 128 - 8 * k, 1), out)
    wells_out[...] = out[0:4, 0:8]

    for copy in started:
        copy.wait_send()
    for r in range(per_dev):
        for dest_j in range(n_gy):
            own, copy = b_copy(r, dest_j)
            pl.when(jnp.logical_not(own))(copy.wait_send)


def per_device(n_gx, n_gy, *args):
    nz = args[5].shape[0]
    a_count = 4 * n_gy
    per_dev = n_gx // a_count
    planes = n_gx // 4
    packs = nz // PACK

    def f32(*lead):
        return pltpu.VMEM((*lead, 8, 128), F32)

    def bf16(*lead):
        return pltpu.VMEM((*lead, 16, 128), BF16)

    dma = pltpu.SemaphoreType.DMA
    vmem = pl.BlockSpec(memory_space=pltpu.VMEM)
    return pl.pallas_call(
        functools.partial(kernel, n_gx, n_gy, nz),
        out_shape=(
            pltpu.VMEM((2, nz, 8, 128), F32),
            pltpu.VMEM((4, 8), F32),
        ),
        in_specs=[pl.BlockSpec(memory_space=pltpu.HBM)] * 11,
        out_specs=(vmem, vmem),
        scratch_shapes=[pltpu.VMEM(a.shape, a.dtype) for a in args] + [
            dma((11,)),
            f32(2, nz), f32(2, nz), f32(2, nz), f32(2, nz), f32(2, nz + 1),
            f32(2, 4, nz), f32(2, 4, nz), f32(4, nz), f32(2, 2, nz), f32(2, 2, nz),
            f32(2, 2, nz + 2), f32(2, 2, nz + 2),
            f32(6, 2), f32(2, 4), f32(2, 4), f32(2, 2), f32(2, 2), f32(2, 2), f32(2, 2),
            bf16(2, 11, packs), f32(2, 2, 2 * packs), bf16(2, 4, packs), f32(2, 2, 2 * packs),
            bf16(2, 11, packs), f32(2, 2, 2 * packs), bf16(2, 4, packs), f32(2, 2, 2 * packs),
            dma((4, 2)), dma((4, 2)),
            bf16(2, 3), f32(2), bf16(2), f32(2),
            bf16(2, 3), f32(2), bf16(2), f32(2),
            dma((4, 2)), dma((4, 2)),
            bf16(4, 2), f32(4), f32(4), bf16(4, 2), f32(4), f32(4),
            dma((4, 4)), dma((4, 4)),
            pltpu.VMEM((256, 256), BF16), pltpu.VMEM((256, 128), F32),
            pltpu.VMEM((n_gx, 1, 128), F32), pltpu.VMEM((n_gx, 1, 128), F32),
            pltpu.VMEM((per_dev, 1, 128), F32), pltpu.VMEM((planes, 1, 128), F32),
            dma((a_count,)), dma, dma((per_dev * n_gy,)), dma,
            pltpu.SemaphoreType.REGULAR((2,)),
        ],
        compiler_params=pltpu.CompilerParams(
            collective_id=0, has_side_effects=True, vmem_limit_bytes=60 * 1024 * 1024
        ),
    )(*args)


def solution(mesh):
    n_gx, n_gy = mesh.shape["gx"], mesh.shape["gy"]
    cells = P(None, None, "gx", "gy")
    faces = P(None, "gx", "gy")
    perfs = P("gx", "gy", None)
    return jax.shard_map(
        functools.partial(per_device, n_gx, n_gy),
        mesh=mesh,
        in_specs=(cells,) * 5 + (faces,) * 3 + (perfs,) * 3,
        out_specs=(cells, P(None, "gx")),
        check_vma=False,
    )
```

```python
import functools

import jax
import jax.numpy as jnp
from jax import lax
from jax.experimental import pallas as pl
from jax.experimental.pallas import tpu as pltpu
from jax.sharding import PartitionSpec as P

MESH = pl.DeviceIdType.MESH
F32 = jnp.float32
BF16 = jnp.bfloat16
PACK = 4
CHUNK = 2
WIDE = 6


def iota(shape, dim):
    return lax.broadcasted_iota(jnp.int32, shape, dim)


def onehot_dot(onehot, x):
    high = x.astype(BF16)
    low = (x - high.astype(F32)).astype(BF16)
    return jnp.dot(onehot, high, preferred_element_type=F32) + jnp.dot(
        onehot, low, preferred_element_type=F32
    )


def sub_of(x):
    return iota(x.shape, x.ndim - 2)


def row_shift(a, b, amount):
    ra, rb = pltpu.roll(a, amount, a.ndim - 2), pltpu.roll(b, amount, b.ndim - 2)
    edge = sub_of(a) == (0 if amount == 1 else 7)
    return jnp.where(edge, rb, ra), jnp.where(edge, ra, rb)


def pack_rows(x):
    x = x.reshape(x.shape[0] // 2, 2, 8, 128)
    even, odd = x[:, 0], pltpu.roll(x[:, 1], 4, 1)
    first = sub_of(even) < 4
    return jnp.where(first, odd, even), jnp.where(first, even, odd)


def unpack_rows(low, high):
    first = sub_of(low) < 4
    even = jnp.where(first, high, low)
    odd = pltpu.roll(jnp.where(first, low, high), 4, 1)
    return jnp.stack([even, odd], 1).reshape(2 * low.shape[0], 8, 128)


def block_system(accum, mob, faces, live=None):
    d = [accum[k] + faces * mob[k] for k in range(4)]
    det = d[0] * d[3] - d[1] * d[2]
    if live is not None:
        det = jnp.where(live, det, 1.0)
    scale = 1.0 / det
    inv = [d[3] * scale, -d[1] * scale, -d[2] * scale, d[0] * scale]
    b = mob
    mat = [
        inv[0] * b[0] + inv[2] * b[1],
        inv[0] * b[2] + inv[2] * b[3],
        inv[1] * b[0] + inv[3] * b[1],
        inv[1] * b[2] + inv[3] * b[3],
    ]
    return inv, mat


def transpose_apply(m, v):
    return [m[0] * v[0] + m[2] * v[1], m[1] * v[0] + m[3] * v[1]]


def kernel(n_gx, n_gy, nz, *refs):
    inputs, (early_out, wells_out), held = refs[:11], refs[11:13], refs[13:24]
    (
        in_sem, tx, txp, ty, typ, tz, k_late, k_early, inv_early, base_late, base_early, y_a, y_b,
        rim_faces, rim_k_late, rim_k_early, rim_late, rim_early, rim_a, rim_b,
        xs_t, xs_bf, xs_f, xs_me, xs_e, xr_t, xr_bf, xr_f, xr_me, xr_e, x_send, x_recv,
        ys_bf, ys_f, ys_me, ys_e, yr_bf, yr_f, yr_me, yr_e, y_send, y_recv,
        zs_bf, zs_f, zs_e, zr_bf, zr_f, zr_e, z_send, z_recv,
        cell_row, col_weight, pbuf, ra, sb, rb, a_send, a_recv, b_send, b_recv, hello,
    ) = refs[24:]
    (
        grad_late, grad_early, accum, mob_late, mob_early, trans_x, trans_y, trans_z,
        perf_cell, perf_well, productivity,
    ) = held
    i = lax.axis_index("gx")
    j = lax.axis_index("gy")
    group = 4
    planes = n_gx // group
    plane, spot = i // group, i % group
    lower, upper = (i + n_gx - 1) % n_gx, (i + 1) % n_gx
    left, right = (j + n_gy - 1) % n_gy, (j + 1) % n_gy
    row_peers = ((upper, j), (lower, j))
    col_peers = ((i, right), (i, left))
    corner_peers = ((upper, right), (upper, left), (lower, right), (lower, left))
    px, py, core = 2 * (j % 2) + spot // 2, j // 2, spot % 2
    offsets = sorted(
        ((dx, dy, dc) for dx in range(4) for dy in range(4) for dc in range(2)),
        key=lambda o: -min(o[0], 4 - o[0]) - min(o[1], 4 - o[1]) - o[2] / 2,
    )[:-1]

    def plane_partner(offset):
        dx, dy, dc = offset
        x, to_core = (px + dx) % 4, core + dc - 2 * core * dc
        to_spot = (x % 2) * 2 + to_core
        return plane * group + to_spot, ((py + dy) % 4) * 2 + x // 2

    plane_partners = [plane_partner(o) for o in offsets]

    loads = [
        pltpu.make_async_copy(inputs[k], held[k], in_sem.at[k])
        for k in (5, 6, 7, 3, 2, 0, 4, 1, 8, 9, 10)
    ]
    for load in loads:
        load.start()

    def mate(distance):
        return ((i + group * distance + n_gx) % n_gx, j)

    near = [mate(d) for d in (-3, -2, -1, 1, 2, 3)]
    far = [mate(d) for d in (-5, 5)]
    barrier = pltpu.get_barrier_semaphore()
    greeted = [*row_peers, *col_peers, *corner_peers, *near] + plane_partners
    for device in greeted:
        pl.semaphore_signal(barrier, inc=1, device_id=device, device_id_type=MESH)
    for load in loads:
        load.wait()

    zero = jnp.zeros((8, 128), F32)
    lane1 = iota((8, 128), 1)
    sub1 = iota((8, 128), 0)
    layer_of = lane1 // WIDE
    col_of = lane1 % WIDE
    live = lane1 < WIDE * nz
    packs = nz // PACK
    steps = nz // CHUNK
    first_row = jnp.where(i == 0, 0, -1)
    first_col = jnp.where(j == 0, 0, -1)

    def pack_cols(old, x, layer, extra=3):
        return jnp.where(layer_of == layer, pltpu.roll(x, extra + WIDE * layer, 1), old)

    def put_rows(x, s, send, k):
        last, first = pack_rows(x)
        if send.dtype == BF16:
            send[0, k, s] = last.reshape(4 * PACK, 128).astype(BF16)
            send[1, k, s] = first.reshape(4 * PACK, 128).astype(BF16)
        else:
            send[0, k, pl.ds(2 * s, 2)] = last
            send[1, k, pl.ds(2 * s, 2)] = first

    def first_out(s, cols):
        at = pl.ds(s * PACK, PACK)
        row, col = iota((PACK, 8, 128), 1), iota((PACK, 8, 128), 2)
        fx = jnp.where(row == first_row, 0.0, trans_x[at].astype(F32))
        fy = jnp.where(col == first_col, 0.0, trans_y[at].astype(F32))
        fz = jnp.where(iota((PACK, 8, 128), 0) + s * PACK == 0, 0.0, trans_z[at].astype(F32))
        tx[0, at] = fx
        ty[0, at] = fy
        tz[0, at] = fz
        fields = [mob_late[k, at].astype(F32) for k in range(4)]
        fields += [accum[k, at].astype(F32) for k in range(4)]
        for k, x in enumerate(fields):
            put_rows(x, s, xs_bf, k)
        fields += [fx, fy, fz]
        for k, x in enumerate(fields[8:]):
            put_rows(x, s, xs_t, k)
        grads = [grad_late[c, at] for c in range(2)]
        for k, x in enumerate(grads):
            put_rows(x, s, xs_f, k)
        early = [mob_early[k, at].astype(F32) for k in range(4)]
        for k, x in enumerate(early):
            put_rows(x, s, xs_me, k)
        cols = list(cols)
        for t in range(PACK):
            layer = s * PACK + t
            for k, x in enumerate(fields + [fy] + grads + early):
                cols[k] = pack_cols(cols[k], x[t], layer, 2 if k == 11 else 3)
        return tuple(cols)

    cols = lax.fori_loop(0, packs, first_out, (zero,) * 18, unroll=5)
    def pair_cols(a, b):
        return (
            jnp.where(col_of < 3, a, pltpu.roll(b, 3, 1)),
            jnp.where(col_of < 3, pltpu.roll(a, 125, 1), b),
        )

    def pair_corners(p, r):
        turned = pltpu.roll(r, 4, 0)
        return jnp.where(sub1 < 4, turned, p), jnp.where(sub1 < 4, p, turned)

    def to_bf(a, b):
        return jnp.concatenate([a, b], 0).astype(BF16)

    pairs = [pair_cols(cols[2 * k], cols[2 * k + 1]) for k in range(9)]
    for side in range(2):
        part = [p[side] for p in pairs]
        for k in range(3):
            ys_bf[side, k] = to_bf(part[2 * k], part[2 * k + 1])
        ys_f[side] = part[6]
        ys_me[side] = to_bf(part[7], part[8])
        order = (0, 1, 2, 3, 4, 5, 7, 8)
        quads = [pair_corners(part[order[2 * k]], part[order[2 * k + 1]]) for k in range(4)]
        for end in range(2):
            for k in range(2):
                zs_bf[2 * end + side, k] = to_bf(quads[2 * k][end], quads[2 * k + 1][end])
            zs_f[2 * end + side] = part[6]

    pl.semaphore_wait(barrier, len(greeted))

    started = []

    def send(kind, *parts):
        copies = []
        for src, dst, peers, sems in parts:
            for k, device in enumerate(peers):
                copies.append(pltpu.make_async_remote_copy(
                    src_ref=src.at[k], dst_ref=dst.at[k], send_sem=sems[0].at[kind, k],
                    recv_sem=sems[1].at[kind, k], device_id=device, device_id_type=MESH,
                ))
        for copy in copies:
            copy.start()
        started.extend(copies)
        return copies

    rows = row_peers, (x_send, x_recv)
    sides = col_peers, (y_send, y_recv)
    corners = corner_peers, (z_send, z_recv)

    def arrived(copies):
        for copy in copies:
            copy.wait_recv()

    sent_t = send(0, (zs_bf, zr_bf, *corners), (ys_bf, yr_bf, *sides), (xs_t, xr_t, *rows))
    sent_f = send(1, (zs_f, zr_f, *corners), (ys_f, yr_f, *sides), (xs_f, xr_f, *rows))
    sent_bf = send(4, (xs_bf, xr_bf, *rows))

    for device in near:
        pl.semaphore_signal(hello.at[0], inc=1, device_id=device, device_id_type=MESH)

    cells = jnp.transpose(jnp.broadcast_to(perf_cell[0], (128, 256)))
    wells = jnp.transpose(jnp.broadcast_to(perf_well[0], (128, 256)))
    prods = jnp.transpose(jnp.broadcast_to(productivity[0], (128, 256)))
    lane_p = iota((256, 128), 1)
    cell_line = cells // 128
    cell_row[:, 0:128] = jnp.where(cell_line == lane_p, 1.0, 0.0).astype(BF16)
    cell_row[:, 128:256] = jnp.where(cell_line == lane_p + 128, 1.0, 0.0).astype(BF16)
    col_weight[...] = jnp.where(cells % 128 == lane_p, prods, 0.0)
    for block in range(2):
        tz[block, nz] = zero
        for buf in (y_a, y_b):
            for c in range(2):
                buf[block, c, 0] = zero
                buf[block, c, nz + 1] = zero

    def get_rows(recv, k, s):
        if recv.dtype == BF16:
            low, high = (recv[d, k, s].astype(F32).reshape(2, 8, 128) for d in range(2))
        else:
            low, high = (recv[d, k, pl.ds(2 * s, 2)] for d in range(2))
        return unpack_rows(low, high)

    def split_cols(a, b):
        return (
            jnp.where(col_of < 3, a, pltpu.roll(b, 3, 1)),
            jnp.where(col_of < 3, pltpu.roll(a, 125, 1), b),
        )

    def halves(tile):
        tile = tile.astype(F32)
        return tile[0:8], tile[8:16]

    def split_rows(down, up):
        return jnp.where(sub1 < 4, up, down), pltpu.roll(jnp.where(sub1 < 4, down, up), 4, 0)

    def rim_fields(y_tiles, z_tiles):
        beside = [split_cols(*pair) for pair in zip(*y_tiles)]
        corner = [split_cols(*pair) for pair in zip(*z_tiles)]
        return [(beside[k // 2][k % 2], corner[k // 2][k % 2]) for k in range(2 * len(beside))]

    def corner_bf(quads):
        tiles = []
        for side in range(2):
            part = []
            for k in quads:
                down, up = (halves(zr_bf[d + side, k // 2])[k % 2] for d in (0, 2))
                part += split_rows(down, up)
            tiles.append(part)
        return tiles

    def corner_f(recv):
        return [[jnp.where(sub1 < 4, recv[2 + side], recv[side])] for side in range(2)]

    arrived(sent_t)

    def rim_trans(s, old):
        at = pl.ds(s * PACK, PACK)
        tx[1, at] = get_rows(xr_t, 0, s)
        fy = get_rows(xr_t, 1, s)
        ty[1, at] = fy
        tz[1, at] = get_rows(xr_t, 2, s)
        for t in range(PACK):
            old = pack_cols(old, fy[t], s * PACK + t)
        return old

    ty_cols = (cols[9], lax.fori_loop(0, packs, rim_trans, zero, unroll=5))
    rim_bf = rim_fields(
        [[h for k in range(3) for h in halves(yr_bf[side, k])] for side in range(2)],
        corner_bf((0, 1, 2)),
    )
    rim_tx, rim_ty, rim_tz, rim_typ = rim_bf[8:12]
    rim_txp = row_shift(*rim_tx, 7)
    rim_all = []
    for block in range(2):
        at_edge = pltpu.roll(ty_cols[block], 127, 1)
        faces = [
            rim_tx[block], rim_txp[block], rim_ty[block],
            jnp.where(col_of == 2, at_edge, rim_typ[block]),
            rim_tz[block], pltpu.roll(rim_tz[block], 128 - WIDE, 1),
        ]
        for k in range(6):
            rim_faces[k, block] = faces[k]
        rim_all.append(faces[0] + faces[1] + faces[2] + faces[3] + faces[4] + faces[5])

    def ends(packed, s):
        return jnp.stack([pltpu.roll(packed, 125 - WIDE * (s * CHUNK + t), 1) for t in range(CHUNK)])

    def late_system(block, cols, step, acc, mob, grad, faces):
        at = pl.ds(step * CHUNK, CHUNK)
        inv, mat = block_system(acc, mob, faces)
        for k in range(4):
            k_late[block, k, at] = mat[k]
        first = transpose_apply(inv, grad)
        for c in range(2):
            base_late[block, c, at] = first[c]
            y_a[block, c, pl.ds(step * CHUNK + 1, CHUNK)] = first[c]
            for t in range(CHUNK):
                cols[c] = pack_cols(cols[c], first[c][t], step * CHUNK + t)

    def own_systems(step, cols):
        cols = list(cols)
        at = pl.ds(step * CHUNK, CHUNK)
        after = pl.ds(step * CHUNK + 1, CHUNK)
        lane = iota((CHUNK, 8, 128), 2)
        far_x = row_shift(tx[0, at], tx[1, at], 7)
        acc = [accum[k, at].astype(F32) for k in range(4)]
        for block in range(2):
            fy = ty[block, at]
            far_y = pltpu.roll(jnp.where(lane == 0, ends(rim_ty[block], step), fy), 127, 2)
            txp[block, at] = far_x[block]
            typ[block, at] = far_y
            if block == 0:
                faces = tx[block, at] + far_x[block] + fy + far_y + tz[block, at] + tz[block, after]
                mob = [mob_late[k, at].astype(F32) for k in range(4)]
                late_system(0, cols, step, acc, mob, [grad_late[c, at] for c in range(2)], faces)
                inv, mat = block_system(acc, [mob_early[k, at].astype(F32) for k in range(4)], faces)
                for k in range(4):
                    k_early[0, k, at] = mat[k]
                    inv_early[k, at] = inv[k]
        return tuple(cols)

    late_own = lax.fori_loop(0, steps, own_systems, (zero, zero), unroll=5)

    def rim_systems(s, cols):
        cols = list(cols)
        mob = [get_rows(xr_bf, k, s) for k in range(4)]
        acc = [get_rows(xr_bf, 4 + k, s) for k in range(4)]
        grad = [get_rows(xr_f, c, s) for c in range(2)]
        for h in range(PACK // CHUNK):
            part = slice(h * CHUNK, (h + 1) * CHUNK)
            step = s * (PACK // CHUNK) + h
            at = pl.ds(step * CHUNK, CHUNK)
            after = pl.ds(step * CHUNK + 1, CHUNK)
            faces = tx[1, at] + txp[1, at] + ty[1, at] + typ[1, at] + tz[1, at] + tz[1, after]
            late_system(1, cols, step, *([x[part] for x in f] for f in (acc, mob, grad)), faces)
        return tuple(cols)

    cols_none = ((zero, zero), (zero, zero))
    arrived(sent_f)
    arrived(sent_bf)
    sent_me = send(2, (ys_me, yr_me, *sides), (xs_me, xr_me, *rows))
    late_cols = (late_own, lax.fori_loop(0, packs, rim_systems, (zero, zero), unroll=5))
    rim_mob_y, rim_acc_y = rim_bf[0:4], rim_bf[4:8]
    rim_grad_y = rim_fields([[yr_f[side]] for side in range(2)], corner_f(zr_f))
    for block in range(2):
        inv, mat = block_system(
            [x[block] for x in rim_acc_y], [x[block] for x in rim_mob_y], rim_all[block], live
        )
        first = transpose_apply(inv, [x[block] for x in rim_grad_y])
        for k in range(4):
            rim_k_late[block, k] = mat[k]
        for c in range(2):
            rim_late[block, c] = first[c]
            rim_a[block, c] = first[c]

    def sweep(cols, y, rim_y, mats, base, rim_mats, rim_base, y_out, rim_out, last=False):
        old = [[rim_y[block, c] for c in range(2)] for block in range(2)]
        blocks = (0,) if last else (0, 1)

        def body(s, packed):
            packed = [list(p) for p in packed]
            at = pl.ds(s * CHUNK, CHUNK)
            at1 = pl.ds(s * CHUNK + 1, CHUNK)
            at2 = pl.ds(s * CHUNK + 2, CHUNK)
            lane = iota((CHUNK, 8, 128), 2)
            flow = [[], []]
            for c in range(2):
                mid = [y[block, c, at1] for block in range(2)]
                below = row_shift(*mid, 1)
                above = row_shift(*mid, 7)
                for block in blocks:
                    side = ends(old[block][c], s)
                    y_low = pltpu.roll(jnp.where(lane == 127, side, mid[block]), 1, 2)
                    y_high = pltpu.roll(jnp.where(lane == 0, side, mid[block]), 127, 2)
                    flow[block].append(
                        tx[block, at] * below[block] + txp[block, at] * above[block]
                        + ty[block, at] * y_low + typ[block, at] * y_high
                        + tz[block, at] * y[block, c, at] + tz[block, at1] * y[block, c, at2]
                    )
            for block in blocks:
                for c in range(2):
                    new = (
                        base[block, c, at] + mats[block, 2 * c, at] * flow[block][0]
                        + mats[block, 2 * c + 1, at] * flow[block][1]
                    )
                    if last:
                        y_out(c, s, new)
                    else:
                        y_out[block, c, at1] = new
                        for t in range(CHUNK):
                            packed[block][c] = pack_cols(packed[block][c], new[t], s * CHUNK + t)
            return tuple(tuple(p) for p in packed)

        packed = lax.fori_loop(0, steps, body, cols_none, unroll=5)
        if last:
            return None
        flow = [[], []]
        for c in range(2):
            below = row_shift(old[0][c], old[1][c], 1)
            above = row_shift(old[0][c], old[1][c], 7)
            for block in range(2):
                mid, own = old[block][c], cols[block][c]
                f = [rim_faces[k, block] for k in range(6)]
                flow[block].append(
                    f[0] * below[block] + f[1] * above[block]
                    + f[2] * pltpu.roll(jnp.where(col_of == 2, own, mid), 1, 1)
                    + f[3] * pltpu.roll(jnp.where(col_of == 3, own, mid), 127, 1)
                    + f[4] * pltpu.roll(mid, WIDE, 1) + f[5] * pltpu.roll(mid, 128 - WIDE, 1)
                )
        for block in range(2):
            for c in range(2):
                rim_out[block, c] = (
                    rim_base[block, c] + rim_mats[block, 2 * c] * flow[block][0]
                    + rim_mats[block, 2 * c + 1] * flow[block][1]
                )
        return packed

    late_args = (k_late, base_late, rim_k_late, rim_late)
    late_cols = sweep(late_cols, y_a, rim_a, *late_args, y_b, rim_b)
    late_cols = sweep(late_cols, y_b, rim_b, *late_args, y_a, rim_a)

    def keep_late(c, s, new):
        y_b[0, c, pl.ds(s * CHUNK + 1, CHUNK)] = new

    sweep(late_cols, y_a, rim_a, *late_args, keep_late, None, last=True)

    def start_early(s, cols):
        cols = list(cols)
        at = pl.ds(s * PACK, PACK)
        at1 = pl.ds(s * PACK + 1, PACK)
        late = [y_b[0, c, at1] for c in range(2)]
        more = transpose_apply([accum[k, at].astype(F32) for k in range(4)], late)
        source = [grad_early[c, at] + more[c] for c in range(2)]
        first = transpose_apply([inv_early[k, at] for k in range(4)], source)
        for c in range(2):
            base_early[0, c, at] = first[c]
            y_a[0, c, at1] = first[c]
            put_rows(first[c], s, xs_e, c)
            for t in range(PACK):
                cols[c] = pack_cols(cols[c], first[c][t], s * PACK + t)
        return tuple(cols)

    own_cols = lax.fori_loop(0, packs, start_early, (zero, zero), unroll=5)
    pair = pair_cols(*own_cols)
    for side in range(2):
        ys_e[side] = pair[side]
        for end in range(2):
            zs_e[2 * end + side] = pair[side]
    sent_e = send(3, (zs_e, zr_e, *corners), (ys_e, yr_e, *sides), (xs_e, xr_e, *rows))

    pl.semaphore_wait(hello.at[0], len(near))
    for device in far:
        pl.semaphore_signal(hello.at[1], inc=1, device_id=device, device_id_type=MESH)
    arrived(sent_me)

    def rim_early_mats(s, _):
        rim_mob = [get_rows(xr_me, k, s) for k in range(4)]
        rim_acc = [get_rows(xr_bf, 4 + k, s) for k in range(4)]
        at = pl.ds(s * PACK, PACK)
        after = pl.ds(s * PACK + 1, PACK)
        faces = tx[1, at] + txp[1, at] + ty[1, at] + typ[1, at] + tz[1, at] + tz[1, after]
        _, mat = block_system(rim_acc, rim_mob, faces)
        for k in range(4):
            k_early[1, k, at] = mat[k]
        return 0

    lax.fori_loop(0, packs, rim_early_mats, 0, unroll=5)
    rim_mob_y = rim_fields([halves(yr_me[side]) for side in range(2)], corner_bf((3,)))
    for block in range(2):
        _, mat = block_system(
            [x[block] for x in rim_acc_y], [x[block] for x in rim_mob_y], rim_all[block], live
        )
        for k in range(4):
            rim_k_early[block, k] = mat[k]

    pad = jnp.zeros((256 - 8 * nz, 128), F32)

    def picked(field):
        lines = jnp.concatenate([field.reshape(8 * nz, 128), pad], 0)
        terms = onehot_dot(cell_row[...], lines) * col_weight[...]
        return jnp.sum(terms, axis=1, keepdims=True)

    own_lane = lane_p - 8 * group * (wells // 8 % group) - wells % 8
    spread = jnp.zeros((256, 128), F32)
    for c in range(2):
        spread = jnp.where(own_lane == 8 * (c + 2), picked(y_b[0, c, pl.ds(1, nz)]), spread)
    owner = jnp.where(
        iota((planes, 256), 0) == jnp.broadcast_to(perf_well[0] // (8 * group), (planes, 256)), 1.0, 0.0
    ).astype(BF16)

    arrived(sent_e)

    def rim_start(s, cols):
        cols = list(cols)
        at = pl.ds(s * PACK, PACK)
        at1 = pl.ds(s * PACK + 1, PACK)
        for c in range(2):
            first = get_rows(xr_e, c, s)
            base_early[1, c, at] = first
            y_a[1, c, at1] = first
            for t in range(PACK):
                cols[c] = pack_cols(cols[c], first[t], s * PACK + t)
        return tuple(cols)

    early_cols = (own_cols, lax.fori_loop(0, packs, rim_start, (zero, zero), unroll=5))
    rim_first = rim_fields([[yr_e[side]] for side in range(2)], corner_f(zr_e))
    for c in range(2):
        pair = rim_first[c]
        for block in range(2):
            rim_early[block, c] = pair[block]
            rim_a[block, c] = pair[block]

    early_args = (k_early, base_early, rim_k_early, rim_early)
    early_cols = sweep(early_cols, y_a, rim_a, *early_args, y_b, rim_b)
    early_cols = sweep(early_cols, y_b, rim_b, *early_args, y_a, rim_a)

    def keep_early(c, s, new):
        early_out[c, pl.ds(s * CHUNK, CHUNK)] = new

    sweep(early_cols, y_a, rim_a, *early_args, keep_early, None, last=True)

    for c in range(2):
        spread = jnp.where(own_lane == 8 * c, picked(early_out[c]), spread)
    partial = onehot_dot(owner, spread)
    for o in range(planes):
        pbuf[o] = partial[o : o + 1]

    pl.semaphore_wait(hello.at[1], len(far))
    for d in range(planes - 1):
        to = d + (d >= plane).astype(jnp.int32)
        place = plane - (plane > to).astype(jnp.int32)
        copy = pltpu.make_async_remote_copy(
            src_ref=pbuf.at[to], dst_ref=ra.at[place],
            send_sem=a_send.at[d], recv_sem=a_recv, device_id=(to * group + spot, j), device_id_type=MESH,
        )
        copy.start()
        started.append(copy)
    pltpu.make_async_copy(ra, ra, a_recv).wait()
    total = pbuf[plane]
    for d in range(planes - 1):
        total = total + ra[d]
    sb[...] = total

    for d, device in enumerate(plane_partners):
        copy = pltpu.make_async_remote_copy(
            src_ref=sb, dst_ref=rb.at[d], send_sem=b_send.at[d], recv_sem=b_recv,
            device_id=device, device_id_type=MESH,
        )
        copy.start()
        started.append(copy)
    for copy in started:
        copy.wait_send()
    pltpu.make_async_copy(rb, rb, b_recv).wait()
    for d in range(len(offsets)):
        total = total + rb[d]
    total = pltpu.roll(jnp.broadcast_to(total, (8, 128)), 128 - 8 * group * spot, 1)
    out = total
    for k in range(1, 4):
        out = jnp.where(sub1 == k, pltpu.roll(total, 128 - 8 * k, 1), out)
    wells_out[...] = out[0:4, 0:8]


def per_device(n_gx, n_gy, *args):
    nz = args[5].shape[0]
    planes = n_gx // 4
    others = 4 * n_gy - 1
    packs = nz // PACK

    def f32(*lead):
        return pltpu.VMEM((*lead, 8, 128), F32)

    def bf16(*lead):
        return pltpu.VMEM((*lead, 16, 128), BF16)

    dma = pltpu.SemaphoreType.DMA
    vmem = pl.BlockSpec(memory_space=pltpu.VMEM)
    return pl.pallas_call(
        functools.partial(kernel, n_gx, n_gy, nz),
        out_shape=(
            pltpu.VMEM((2, nz, 8, 128), F32),
            pltpu.VMEM((4, 8), F32),
        ),
        in_specs=[pl.BlockSpec(memory_space=pltpu.HBM)] * 11,
        out_specs=(vmem, vmem),
        scratch_shapes=[pltpu.VMEM(a.shape, a.dtype) for a in args] + [
            dma((11,)),
            f32(2, nz), f32(2, nz), f32(2, nz), f32(2, nz), f32(2, nz + 1),
            f32(2, 4, nz), f32(2, 4, nz), f32(4, nz), f32(2, 2, nz), f32(2, 2, nz),
            f32(2, 2, nz + 2), f32(2, 2, nz + 2),
            f32(6, 2), f32(2, 4), f32(2, 4), f32(2, 2), f32(2, 2), f32(2, 2), f32(2, 2),
            bf16(2, 3, packs), bf16(2, 8, packs), f32(2, 2, 2 * packs), bf16(2, 4, packs), f32(2, 2, 2 * packs),
            bf16(2, 3, packs), bf16(2, 8, packs), f32(2, 2, 2 * packs), bf16(2, 4, packs), f32(2, 2, 2 * packs),
            dma((5, 2)), dma((5, 2)),
            bf16(2, 3), f32(2), bf16(2), f32(2),
            bf16(2, 3), f32(2), bf16(2), f32(2),
            dma((4, 2)), dma((4, 2)),
            bf16(4, 2), f32(4), f32(4), bf16(4, 2), f32(4), f32(4),
            dma((4, 4)), dma((4, 4)),
            pltpu.VMEM((256, 256), BF16), pltpu.VMEM((256, 128), F32),
            pltpu.VMEM((planes, 1, 128), F32), pltpu.VMEM((planes - 1, 1, 128), F32),
            pltpu.VMEM((1, 128), F32), pltpu.VMEM((others, 1, 128), F32),
            dma((planes - 1,)), dma, dma((others,)), dma,
            pltpu.SemaphoreType.REGULAR((2,)),
        ],
        compiler_params=pltpu.CompilerParams(
            collective_id=0, has_side_effects=True, vmem_limit_bytes=60 * 1024 * 1024
        ),
    )(*args)


def solution(mesh):
    n_gx, n_gy = mesh.shape["gx"], mesh.shape["gy"]
    cells = P(None, None, "gx", "gy")
    faces = P(None, "gx", "gy")
    perfs = P("gx", "gy", None)
    return jax.shard_map(
        functools.partial(per_device, n_gx, n_gy),
        mesh=mesh,
        in_specs=(cells,) * 5 + (faces,) * 3 + (perfs,) * 3,
        out_specs=(cells, P(None, "gx")),
        check_vma=False,
    )
```

```python
import functools

import jax
import jax.numpy as jnp
from jax import lax
from jax.experimental import pallas as pl
from jax.experimental.pallas import tpu as pltpu
from jax.sharding import PartitionSpec as P

MESH = pl.DeviceIdType.MESH
F32 = jnp.float32
BF16 = jnp.bfloat16
PACK = 4
CHUNK = 4
WIDE = 6


def iota(shape, dim):
    return lax.broadcasted_iota(jnp.int32, shape, dim)


def onehot_dot(onehot, x):
    high = x.astype(BF16)
    low = (x - high.astype(F32)).astype(BF16)
    return jnp.dot(onehot, high, preferred_element_type=F32) + jnp.dot(
        onehot, low, preferred_element_type=F32
    )


def sub_of(x):
    return iota(x.shape, x.ndim - 2)


def row_shift(a, b, amount):
    ra, rb = pltpu.roll(a, amount, a.ndim - 2), pltpu.roll(b, amount, b.ndim - 2)
    edge = sub_of(a) == (0 if amount == 1 else 7)
    return jnp.where(edge, rb, ra), jnp.where(edge, ra, rb)


def pack_rows(x):
    x = x.reshape(x.shape[0] // 2, 2, 8, 128)
    even, odd = x[:, 0], pltpu.roll(x[:, 1], 4, 1)
    first = sub_of(even) < 4
    return jnp.where(first, odd, even), jnp.where(first, even, odd)


def unpack_rows(low, high):
    first = sub_of(low) < 4
    even = jnp.where(first, high, low)
    odd = pltpu.roll(jnp.where(first, low, high), 4, 1)
    return jnp.stack([even, odd], 1).reshape(2 * low.shape[0], 8, 128)


def block_system(accum, mob, faces, live=None):
    d = [accum[k] + faces * mob[k] for k in range(4)]
    det = d[0] * d[3] - d[1] * d[2]
    if live is not None:
        det = jnp.where(live, det, 1.0)
    scale = 1.0 / det
    inv = [d[3] * scale, -d[1] * scale, -d[2] * scale, d[0] * scale]
    b = mob
    mat = [
        inv[0] * b[0] + inv[2] * b[1],
        inv[0] * b[2] + inv[2] * b[3],
        inv[1] * b[0] + inv[3] * b[1],
        inv[1] * b[2] + inv[3] * b[3],
    ]
    return inv, mat


def transpose_apply(m, v):
    return [m[0] * v[0] + m[2] * v[1], m[1] * v[0] + m[3] * v[1]]


def kernel(n_gx, n_gy, nz, *refs):
    inputs, (early_out, wells_out), held = refs[:11], refs[11:13], refs[13:24]
    (
        in_sem, tx, txp, ty, typ, tz, k_late, k_early, inv_early, base_late, base_early, y_a, y_b,
        rim_faces, rim_k_late, rim_k_early, rim_late, rim_early, rim_a, rim_b,
        xs_t, xs_bf, xs_f, xs_me, xs_e, xr_t, xr_bf, xr_f, xr_me, xr_e, x_send, x_recv,
        ys_bf, ys_f, ys_me, ys_e, yr_bf, yr_f, yr_me, yr_e, y_send, y_recv,
        zs_bf, zs_f, zs_e, zr_bf, zr_f, zr_e, z_send, z_recv,
        cell_row, col_weight, pbuf, ra, sb, rb, a_send, a_recv, b_send, b_recv, hello,
    ) = refs[24:]
    (
        grad_late, grad_early, accum, mob_late, mob_early, trans_x, trans_y, trans_z,
        perf_cell, perf_well, productivity,
    ) = held
    i = lax.axis_index("gx")
    j = lax.axis_index("gy")
    group = 4
    planes = n_gx // group
    plane, spot = i // group, i % group
    lower, upper = (i + n_gx - 1) % n_gx, (i + 1) % n_gx
    left, right = (j + n_gy - 1) % n_gy, (j + 1) % n_gy
    row_peers = ((upper, j), (lower, j))
    col_peers = ((i, right), (i, left))
    corner_peers = ((upper, right), (upper, left), (lower, right), (lower, left))
    px, py, core = 2 * (j % 2) + spot // 2, j // 2, spot % 2
    offsets = sorted(
        ((dx, dy, dc) for dx in range(4) for dy in range(4) for dc in range(2)),
        key=lambda o: -min(o[0], 4 - o[0]) - min(o[1], 4 - o[1]) - o[2] / 2,
    )[:-1]

    def plane_partner(offset):
        dx, dy, dc = offset
        x, to_core = (px + dx) % 4, core + dc - 2 * core * dc
        to_spot = (x % 2) * 2 + to_core
        return plane * group + to_spot, ((py + dy) % 4) * 2 + x // 2

    plane_partners = [plane_partner(o) for o in offsets]

    loads = [
        pltpu.make_async_copy(inputs[k], held[k], in_sem.at[k])
        for k in (5, 6, 7, 3, 2, 0, 4, 1, 8, 9, 10)
    ]
    for load in loads:
        load.start()

    def mate(distance):
        return ((i + group * distance + n_gx) % n_gx, j)

    near = [mate(d) for d in (-3, -2, -1, 1, 2, 3)]
    far = [mate(d) for d in (-5, 5)]
    barrier = pltpu.get_barrier_semaphore()
    greeted = [*row_peers, *col_peers, *corner_peers, *near] + plane_partners
    for device in greeted:
        pl.semaphore_signal(barrier, inc=1, device_id=device, device_id_type=MESH)
    for load in loads:
        load.wait()

    zero = jnp.zeros((8, 128), F32)
    lane1 = iota((8, 128), 1)
    sub1 = iota((8, 128), 0)
    layer_of = lane1 // WIDE
    col_of = lane1 % WIDE
    live = lane1 < WIDE * nz
    packs = nz // PACK
    steps = nz // CHUNK
    first_row = jnp.where(i == 0, 0, -1)
    first_col = jnp.where(j == 0, 0, -1)

    def pack_cols(old, x, layer, extra=3):
        return jnp.where(layer_of == layer, pltpu.roll(x, extra + WIDE * layer, 1), old)

    def put_rows(x, s, send, k):
        last, first = pack_rows(x)
        if send.dtype == BF16:
            send[0, k, s] = last.reshape(4 * PACK, 128).astype(BF16)
            send[1, k, s] = first.reshape(4 * PACK, 128).astype(BF16)
        else:
            send[0, k, pl.ds(2 * s, 2)] = last
            send[1, k, pl.ds(2 * s, 2)] = first

    def first_out(s, cols):
        at = pl.ds(s * PACK, PACK)
        row, col = iota((PACK, 8, 128), 1), iota((PACK, 8, 128), 2)
        fx = jnp.where(row == first_row, 0.0, trans_x[at].astype(F32))
        fy = jnp.where(col == first_col, 0.0, trans_y[at].astype(F32))
        fz = jnp.where(iota((PACK, 8, 128), 0) + s * PACK == 0, 0.0, trans_z[at].astype(F32))
        tx[0, at] = fx
        ty[0, at] = fy
        tz[0, at] = fz
        fields = [mob_late[k, at].astype(F32) for k in range(4)]
        fields += [accum[k, at].astype(F32) for k in range(4)]
        for k, x in enumerate(fields):
            put_rows(x, s, xs_bf, k)
        fields += [fx, fy, fz]
        for k, x in enumerate(fields[8:]):
            put_rows(x, s, xs_t, k)
        grads = [grad_late[c, at] for c in range(2)]
        for k, x in enumerate(grads):
            put_rows(x, s, xs_f, k)
        early = [mob_early[k, at].astype(F32) for k in range(4)]
        for k, x in enumerate(early):
            put_rows(x, s, xs_me, k)
        cols = list(cols)
        for t in range(PACK):
            layer = s * PACK + t
            for k, x in enumerate(fields + [fy] + grads + early):
                cols[k] = pack_cols(cols[k], x[t], layer, 2 if k == 11 else 3)
        return tuple(cols)

    cols = lax.fori_loop(0, packs, first_out, (zero,) * 18, unroll=5)
    def pair_cols(a, b):
        return (
            jnp.where(col_of < 3, a, pltpu.roll(b, 3, 1)),
            jnp.where(col_of < 3, pltpu.roll(a, 125, 1), b),
        )

    def pair_corners(p, r):
        turned = pltpu.roll(r, 4, 0)
        return jnp.where(sub1 < 4, turned, p), jnp.where(sub1 < 4, p, turned)

    def to_bf(a, b):
        return jnp.concatenate([a, b], 0).astype(BF16)

    pairs = [pair_cols(cols[2 * k], cols[2 * k + 1]) for k in range(9)]
    for side in range(2):
        part = [p[side] for p in pairs]
        for k in range(3):
            ys_bf[side, k] = to_bf(part[2 * k], part[2 * k + 1])
        ys_f[side] = part[6]
        ys_me[side] = to_bf(part[7], part[8])
        order = (0, 1, 2, 3, 4, 5, 7, 8)
        quads = [pair_corners(part[order[2 * k]], part[order[2 * k + 1]]) for k in range(4)]
        for end in range(2):
            for k in range(2):
                zs_bf[2 * end + side, k] = to_bf(quads[2 * k][end], quads[2 * k + 1][end])
            zs_f[2 * end + side] = part[6]

    pl.semaphore_wait(barrier, len(greeted))

    started = []

    def send(kind, *parts):
        copies = []
        for src, dst, peers, sems in parts:
            for k, device in enumerate(peers):
                copies.append(pltpu.make_async_remote_copy(
                    src_ref=src.at[k], dst_ref=dst.at[k], send_sem=sems[0].at[kind, k],
                    recv_sem=sems[1].at[kind, k], device_id=device, device_id_type=MESH,
                ))
        for copy in copies:
            copy.start()
        started.extend(copies)
        return copies

    rows = row_peers, (x_send, x_recv)
    sides = col_peers, (y_send, y_recv)
    corners = corner_peers, (z_send, z_recv)

    def arrived(copies):
        for copy in copies:
            copy.wait_recv()

    sent_t = send(0, (zs_bf, zr_bf, *corners), (ys_bf, yr_bf, *sides), (xs_t, xr_t, *rows))
    sent_f = send(1, (zs_f, zr_f, *corners), (ys_f, yr_f, *sides), (xs_f, xr_f, *rows))
    sent_bf = send(4, (xs_bf, xr_bf, *rows))

    for device in near:
        pl.semaphore_signal(hello.at[0], inc=1, device_id=device, device_id_type=MESH)

    cells = jnp.transpose(jnp.broadcast_to(perf_cell[0], (128, 256)))
    wells = jnp.transpose(jnp.broadcast_to(perf_well[0], (128, 256)))
    prods = jnp.transpose(jnp.broadcast_to(productivity[0], (128, 256)))
    lane_p = iota((256, 128), 1)
    cell_line = cells // 128
    cell_row[:, 0:128] = jnp.where(cell_line == lane_p, 1.0, 0.0).astype(BF16)
    cell_row[:, 128:256] = jnp.where(cell_line == lane_p + 128, 1.0, 0.0).astype(BF16)
    col_weight[...] = jnp.where(cells % 128 == lane_p, prods, 0.0)
    for block in range(2):
        tz[block, nz] = zero
        for buf in (y_a, y_b):
            for c in range(2):
                buf[block, c, 0] = zero
                buf[block, c, nz + 1] = zero

    def get_rows(recv, k, s):
        if recv.dtype == BF16:
            low, high = (recv[d, k, s].astype(F32).reshape(2, 8, 128) for d in range(2))
        else:
            low, high = (recv[d, k, pl.ds(2 * s, 2)] for d in range(2))
        return unpack_rows(low, high)

    def split_cols(a, b):
        return (
            jnp.where(col_of < 3, a, pltpu.roll(b, 3, 1)),
            jnp.where(col_of < 3, pltpu.roll(a, 125, 1), b),
        )

    def halves(tile):
        tile = tile.astype(F32)
        return tile[0:8], tile[8:16]

    def split_rows(down, up):
        return jnp.where(sub1 < 4, up, down), pltpu.roll(jnp.where(sub1 < 4, down, up), 4, 0)

    def rim_fields(y_tiles, z_tiles):
        beside = [split_cols(*pair) for pair in zip(*y_tiles)]
        corner = [split_cols(*pair) for pair in zip(*z_tiles)]
        return [(beside[k // 2][k % 2], corner[k // 2][k % 2]) for k in range(2 * len(beside))]

    def corner_bf(quads):
        tiles = []
        for side in range(2):
            part = []
            for k in quads:
                down, up = (halves(zr_bf[d + side, k // 2])[k % 2] for d in (0, 2))
                part += split_rows(down, up)
            tiles.append(part)
        return tiles

    def corner_f(recv):
        return [[jnp.where(sub1 < 4, recv[2 + side], recv[side])] for side in range(2)]

    arrived(sent_t)

    def rim_trans(s, old):
        at = pl.ds(s * PACK, PACK)
        tx[1, at] = get_rows(xr_t, 0, s)
        fy = get_rows(xr_t, 1, s)
        ty[1, at] = fy
        tz[1, at] = get_rows(xr_t, 2, s)
        for t in range(PACK):
            old = pack_cols(old, fy[t], s * PACK + t)
        return old

    ty_cols = (cols[9], lax.fori_loop(0, packs, rim_trans, zero, unroll=5))
    rim_bf = rim_fields(
        [[h for k in range(3) for h in halves(yr_bf[side, k])] for side in range(2)],
        corner_bf((0, 1, 2)),
    )
    rim_tx, rim_ty, rim_tz, rim_typ = rim_bf[8:12]
    rim_txp = row_shift(*rim_tx, 7)
    rim_all = []
    for block in range(2):
        at_edge = pltpu.roll(ty_cols[block], 127, 1)
        faces = [
            rim_tx[block], rim_txp[block], rim_ty[block],
            jnp.where(col_of == 2, at_edge, rim_typ[block]),
            rim_tz[block], pltpu.roll(rim_tz[block], 128 - WIDE, 1),
        ]
        for k in range(6):
            rim_faces[k, block] = faces[k]
        rim_all.append(faces[0] + faces[1] + faces[2] + faces[3] + faces[4] + faces[5])

    def ends(packed, s):
        return jnp.stack([pltpu.roll(packed, 125 - WIDE * (s * CHUNK + t), 1) for t in range(CHUNK)])

    def late_system(block, cols, step, acc, mob, grad, faces):
        at = pl.ds(step * CHUNK, CHUNK)
        inv, mat = block_system(acc, mob, faces)
        for k in range(4):
            k_late[block, k, at] = mat[k]
        first = transpose_apply(inv, grad)
        for c in range(2):
            base_late[block, c, at] = first[c]
            y_a[block, c, pl.ds(step * CHUNK + 1, CHUNK)] = first[c]
            for t in range(CHUNK):
                cols[c] = pack_cols(cols[c], first[c][t], step * CHUNK + t)

    def own_systems(step, cols):
        cols = list(cols)
        at = pl.ds(step * CHUNK, CHUNK)
        after = pl.ds(step * CHUNK + 1, CHUNK)
        lane = iota((CHUNK, 8, 128), 2)
        far_x = row_shift(tx[0, at], tx[1, at], 7)
        acc = [accum[k, at].astype(F32) for k in range(4)]
        for block in range(2):
            fy = ty[block, at]
            far_y = pltpu.roll(jnp.where(lane == 0, ends(rim_ty[block], step), fy), 127, 2)
            txp[block, at] = far_x[block]
            typ[block, at] = far_y
            if block == 0:
                faces = tx[block, at] + far_x[block] + fy + far_y + tz[block, at] + tz[block, after]
                mob = [mob_late[k, at].astype(F32) for k in range(4)]
                late_system(0, cols, step, acc, mob, [grad_late[c, at] for c in range(2)], faces)
                inv, mat = block_system(acc, [mob_early[k, at].astype(F32) for k in range(4)], faces)
                for k in range(4):
                    k_early[0, k, at] = mat[k]
                    inv_early[k, at] = inv[k]
        return tuple(cols)

    late_own = lax.fori_loop(0, steps, own_systems, (zero, zero), unroll=5)

    def rim_systems(s, cols):
        cols = list(cols)
        mob = [get_rows(xr_bf, k, s) for k in range(4)]
        acc = [get_rows(xr_bf, 4 + k, s) for k in range(4)]
        grad = [get_rows(xr_f, c, s) for c in range(2)]
        for h in range(PACK // CHUNK):
            part = slice(h * CHUNK, (h + 1) * CHUNK)
            step = s * (PACK // CHUNK) + h
            at = pl.ds(step * CHUNK, CHUNK)
            after = pl.ds(step * CHUNK + 1, CHUNK)
            faces = tx[1, at] + txp[1, at] + ty[1, at] + typ[1, at] + tz[1, at] + tz[1, after]
            late_system(1, cols, step, *([x[part] for x in f] for f in (acc, mob, grad)), faces)
        return tuple(cols)

    cols_none = ((zero, zero), (zero, zero))
    arrived(sent_f)
    arrived(sent_bf)
    pl.semaphore_wait(hello.at[0], len(near))
    for device in far:
        pl.semaphore_signal(hello.at[1], inc=1, device_id=device, device_id_type=MESH)
    sent_me = send(2, (ys_me, yr_me, *sides), (xs_me, xr_me, *rows))
    late_cols = (late_own, lax.fori_loop(0, packs, rim_systems, (zero, zero), unroll=5))
    rim_mob_y, rim_acc_y = rim_bf[0:4], rim_bf[4:8]
    rim_grad_y = rim_fields([[yr_f[side]] for side in range(2)], corner_f(zr_f))
    for block in range(2):
        inv, mat = block_system(
            [x[block] for x in rim_acc_y], [x[block] for x in rim_mob_y], rim_all[block], live
        )
        first = transpose_apply(inv, [x[block] for x in rim_grad_y])
        for k in range(4):
            rim_k_late[block, k] = mat[k]
        for c in range(2):
            rim_late[block, c] = first[c]
            rim_a[block, c] = first[c]

    def sweep(cols, y, rim_y, mats, base, rim_mats, rim_base, y_out, rim_out, last=False):
        old = [[rim_y[block, c] for c in range(2)] for block in range(2)]
        blocks = (0,) if last else (0, 1)

        def body(s, packed):
            packed = [list(p) for p in packed]
            at = pl.ds(s * CHUNK, CHUNK)
            at1 = pl.ds(s * CHUNK + 1, CHUNK)
            at2 = pl.ds(s * CHUNK + 2, CHUNK)
            lane = iota((CHUNK, 8, 128), 2)
            flow = [[], []]
            for c in range(2):
                mid = [y[block, c, at1] for block in range(2)]
                below = row_shift(*mid, 1)
                above = row_shift(*mid, 7)
                for block in blocks:
                    side = ends(old[block][c], s)
                    y_low = pltpu.roll(jnp.where(lane == 127, side, mid[block]), 1, 2)
                    y_high = pltpu.roll(jnp.where(lane == 0, side, mid[block]), 127, 2)
                    flow[block].append(
                        tx[block, at] * below[block] + txp[block, at] * above[block]
                        + ty[block, at] * y_low + typ[block, at] * y_high
                        + tz[block, at] * y[block, c, at] + tz[block, at1] * y[block, c, at2]
                    )
            for block in blocks:
                for c in range(2):
                    new = (
                        base[block, c, at] + mats[block, 2 * c, at] * flow[block][0]
                        + mats[block, 2 * c + 1, at] * flow[block][1]
                    )
                    if last:
                        y_out(c, s, new)
                    else:
                        y_out[block, c, at1] = new
                        for t in range(CHUNK):
                            packed[block][c] = pack_cols(packed[block][c], new[t], s * CHUNK + t)
            return tuple(tuple(p) for p in packed)

        packed = lax.fori_loop(0, steps, body, cols_none, unroll=5)
        if last:
            return None
        flow = [[], []]
        for c in range(2):
            below = row_shift(old[0][c], old[1][c], 1)
            above = row_shift(old[0][c], old[1][c], 7)
            for block in range(2):
                mid, own = old[block][c], cols[block][c]
                f = [rim_faces[k, block] for k in range(6)]
                flow[block].append(
                    f[0] * below[block] + f[1] * above[block]
                    + f[2] * pltpu.roll(jnp.where(col_of == 2, own, mid), 1, 1)
                    + f[3] * pltpu.roll(jnp.where(col_of == 3, own, mid), 127, 1)
                    + f[4] * pltpu.roll(mid, WIDE, 1) + f[5] * pltpu.roll(mid, 128 - WIDE, 1)
                )
        for block in range(2):
            for c in range(2):
                rim_out[block, c] = (
                    rim_base[block, c] + rim_mats[block, 2 * c] * flow[block][0]
                    + rim_mats[block, 2 * c + 1] * flow[block][1]
                )
        return packed

    late_args = (k_late, base_late, rim_k_late, rim_late)
    late_cols = sweep(late_cols, y_a, rim_a, *late_args, y_b, rim_b)
    late_cols = sweep(late_cols, y_b, rim_b, *late_args, y_a, rim_a)

    def keep_late(c, s, new):
        y_b[0, c, pl.ds(s * CHUNK + 1, CHUNK)] = new

    sweep(late_cols, y_a, rim_a, *late_args, keep_late, None, last=True)

    def start_early(s, cols):
        cols = list(cols)
        at = pl.ds(s * PACK, PACK)
        at1 = pl.ds(s * PACK + 1, PACK)
        late = [y_b[0, c, at1] for c in range(2)]
        more = transpose_apply([accum[k, at].astype(F32) for k in range(4)], late)
        source = [grad_early[c, at] + more[c] for c in range(2)]
        first = transpose_apply([inv_early[k, at] for k in range(4)], source)
        for c in range(2):
            base_early[0, c, at] = first[c]
            y_a[0, c, at1] = first[c]
            put_rows(first[c], s, xs_e, c)
            for t in range(PACK):
                cols[c] = pack_cols(cols[c], first[c][t], s * PACK + t)
        return tuple(cols)

    own_cols = lax.fori_loop(0, packs, start_early, (zero, zero), unroll=5)
    pair = pair_cols(*own_cols)
    for side in range(2):
        ys_e[side] = pair[side]
        for end in range(2):
            zs_e[2 * end + side] = pair[side]
    sent_e = send(3, (zs_e, zr_e, *corners), (ys_e, yr_e, *sides), (xs_e, xr_e, *rows))

    arrived(sent_me)

    def rim_early_mats(s, _):
        rim_mob = [get_rows(xr_me, k, s) for k in range(4)]
        rim_acc = [get_rows(xr_bf, 4 + k, s) for k in range(4)]
        at = pl.ds(s * PACK, PACK)
        after = pl.ds(s * PACK + 1, PACK)
        faces = tx[1, at] + txp[1, at] + ty[1, at] + typ[1, at] + tz[1, at] + tz[1, after]
        _, mat = block_system(rim_acc, rim_mob, faces)
        for k in range(4):
            k_early[1, k, at] = mat[k]
        return 0

    lax.fori_loop(0, packs, rim_early_mats, 0, unroll=5)
    rim_mob_y = rim_fields([halves(yr_me[side]) for side in range(2)], corner_bf((3,)))
    for block in range(2):
        _, mat = block_system(
            [x[block] for x in rim_acc_y], [x[block] for x in rim_mob_y], rim_all[block], live
        )
        for k in range(4):
            rim_k_early[block, k] = mat[k]

    pad = jnp.zeros((256 - 8 * nz, 128), F32)

    def picked(field):
        lines = jnp.concatenate([field.reshape(8 * nz, 128), pad], 0)
        terms = onehot_dot(cell_row[...], lines) * col_weight[...]
        return jnp.sum(terms, axis=1, keepdims=True)

    own_lane = lane_p - 8 * group * (wells // 8 % group) - wells % 8
    spread = jnp.zeros((256, 128), F32)
    for c in range(2):
        spread = jnp.where(own_lane == 8 * (c + 2), picked(y_b[0, c, pl.ds(1, nz)]), spread)
    owner = jnp.where(
        iota((planes, 256), 0) == jnp.broadcast_to(perf_well[0] // (8 * group), (planes, 256)), 1.0, 0.0
    ).astype(BF16)

    arrived(sent_e)

    def rim_start(s, cols):
        cols = list(cols)
        at = pl.ds(s * PACK, PACK)
        at1 = pl.ds(s * PACK + 1, PACK)
        for c in range(2):
            first = get_rows(xr_e, c, s)
            base_early[1, c, at] = first
            y_a[1, c, at1] = first
            for t in range(PACK):
                cols[c] = pack_cols(cols[c], first[t], s * PACK + t)
        return tuple(cols)

    early_cols = (own_cols, lax.fori_loop(0, packs, rim_start, (zero, zero), unroll=5))
    rim_first = rim_fields([[yr_e[side]] for side in range(2)], corner_f(zr_e))
    for c in range(2):
        pair = rim_first[c]
        for block in range(2):
            rim_early[block, c] = pair[block]
            rim_a[block, c] = pair[block]

    early_args = (k_early, base_early, rim_k_early, rim_early)
    early_cols = sweep(early_cols, y_a, rim_a, *early_args, y_b, rim_b)
    early_cols = sweep(early_cols, y_b, rim_b, *early_args, y_a, rim_a)

    def keep_early(c, s, new):
        early_out[c, pl.ds(s * CHUNK, CHUNK)] = new

    sweep(early_cols, y_a, rim_a, *early_args, keep_early, None, last=True)

    for c in range(2):
        spread = jnp.where(own_lane == 8 * c, picked(early_out[c]), spread)
    partial = onehot_dot(owner, spread)
    for o in range(planes):
        pbuf[o] = partial[o : o + 1]

    pl.semaphore_wait(hello.at[1], len(far))
    farthest = sorted(range(1, planes), key=lambda o: -min(o, planes - o))
    for d, offset in enumerate(farthest):
        to, place = (plane + offset) % planes, d
        copy = pltpu.make_async_remote_copy(
            src_ref=pbuf.at[to], dst_ref=ra.at[place],
            send_sem=a_send.at[d], recv_sem=a_recv, device_id=(to * group + spot, j), device_id_type=MESH,
        )
        copy.start()
        started.append(copy)
    pltpu.make_async_copy(ra, ra, a_recv).wait()
    total = pbuf[plane]
    for d in range(planes - 1):
        total = total + ra[d]
    sb[...] = total

    for d, device in enumerate(plane_partners):
        copy = pltpu.make_async_remote_copy(
            src_ref=sb, dst_ref=rb.at[d], send_sem=b_send.at[d], recv_sem=b_recv,
            device_id=device, device_id_type=MESH,
        )
        copy.start()
        started.append(copy)
    for copy in started:
        copy.wait_send()
    pltpu.make_async_copy(rb, rb, b_recv).wait()
    for d in range(len(offsets)):
        total = total + rb[d]
    total = pltpu.roll(jnp.broadcast_to(total, (8, 128)), 128 - 8 * group * spot, 1)
    out = total
    for k in range(1, 4):
        out = jnp.where(sub1 == k, pltpu.roll(total, 128 - 8 * k, 1), out)
    wells_out[...] = out[0:4, 0:8]


def per_device(n_gx, n_gy, *args):
    nz = args[5].shape[0]
    planes = n_gx // 4
    others = 4 * n_gy - 1
    packs = nz // PACK

    def f32(*lead):
        return pltpu.VMEM((*lead, 8, 128), F32)

    def bf16(*lead):
        return pltpu.VMEM((*lead, 16, 128), BF16)

    dma = pltpu.SemaphoreType.DMA
    vmem = pl.BlockSpec(memory_space=pltpu.VMEM)
    return pl.pallas_call(
        functools.partial(kernel, n_gx, n_gy, nz),
        out_shape=(
            pltpu.VMEM((2, nz, 8, 128), F32),
            pltpu.VMEM((4, 8), F32),
        ),
        in_specs=[pl.BlockSpec(memory_space=pltpu.HBM)] * 11,
        out_specs=(vmem, vmem),
        scratch_shapes=[pltpu.VMEM(a.shape, a.dtype) for a in args] + [
            dma((11,)),
            f32(2, nz), f32(2, nz), f32(2, nz), f32(2, nz), f32(2, nz + 1),
            f32(2, 4, nz), f32(2, 4, nz), f32(4, nz), f32(2, 2, nz), f32(2, 2, nz),
            f32(2, 2, nz + 2), f32(2, 2, nz + 2),
            f32(6, 2), f32(2, 4), f32(2, 4), f32(2, 2), f32(2, 2), f32(2, 2), f32(2, 2),
            bf16(2, 3, packs), bf16(2, 8, packs), f32(2, 2, 2 * packs), bf16(2, 4, packs), f32(2, 2, 2 * packs),
            bf16(2, 3, packs), bf16(2, 8, packs), f32(2, 2, 2 * packs), bf16(2, 4, packs), f32(2, 2, 2 * packs),
            dma((5, 2)), dma((5, 2)),
            bf16(2, 3), f32(2), bf16(2), f32(2),
            bf16(2, 3), f32(2), bf16(2), f32(2),
            dma((4, 2)), dma((4, 2)),
            bf16(4, 2), f32(4), f32(4), bf16(4, 2), f32(4), f32(4),
            dma((4, 4)), dma((4, 4)),
            pltpu.VMEM((256, 256), BF16), pltpu.VMEM((256, 128), F32),
            pltpu.VMEM((planes, 1, 128), F32), pltpu.VMEM((planes - 1, 1, 128), F32),
            pltpu.VMEM((1, 128), F32), pltpu.VMEM((others, 1, 128), F32),
            dma((planes - 1,)), dma, dma((others,)), dma,
            pltpu.SemaphoreType.REGULAR((2,)),
        ],
        compiler_params=pltpu.CompilerParams(
            collective_id=0, has_side_effects=True, vmem_limit_bytes=60 * 1024 * 1024
        ),
    )(*args)


def solution(mesh):
    n_gx, n_gy = mesh.shape["gx"], mesh.shape["gy"]
    cells = P(None, None, "gx", "gy")
    faces = P(None, "gx", "gy")
    perfs = P("gx", "gy", None)
    return jax.shard_map(
        functools.partial(per_device, n_gx, n_gy),
        mesh=mesh,
        in_specs=(cells,) * 5 + (faces,) * 3 + (perfs,) * 3,
        out_specs=(cells, P(None, "gx")),
        check_vma=False,
    )
```
